128 devices in a mesh: dp: 64 (over z, x_lo, y, core), fsdp: 2 (over x_hi).
Axes of the slice: x: 4 (x_hi: 2, x_lo: 2; x = x_hi * 2 + x_lo), y: 4, z: 4, core: 2. Of those that a mesh axis runs over, the one named last changes fastest.
Arguments:
- tokens: bfloat16 [128, 256, 384], P(('dp', 'fsdp')), may hold values from -24 to 24
- condition: bfloat16 [128, 384], P(('dp', 'fsdp')), may hold values from -24 to 24
- modulation_weight: bfloat16 [1, 384, 2304], P(None, ('dp', 'fsdp')), may hold values from -0.3125 to 0.3125
- modulation_bias: bfloat16 [1, 2304], P(None, ('dp', 'fsdp')), may hold values from -3 to 3
- attend_weight: bfloat16 [1, 384, 1152], P(None, ('dp', 'fsdp')), may hold values from -0.3125 to 0.3125
- attend_bias: bfloat16 [1, 768], P(None, ('dp', 'fsdp')), may hold values from -3 to 3
- output_weight: bfloat16 [1, 384, 384], P(None, ('dp', 'fsdp')), may hold values from -1.25 to 1.25
- output_bias: bfloat16 [1, 384], P(None, ('dp', 'fsdp')), may hold values from -2 to 2
- up_weight: bfloat16 [1, 384, 1536], P(None, ('dp', 'fsdp')), may hold values from -0.3125 to 0.3125
- up_bias: bfloat16 [1, 1536], P(None, ('dp', 'fsdp')), may hold values from -3 to 3
- down_weight: bfloat16 [1, 1536, 384], P(None, ('dp', 'fsdp')), may hold values from -0.15625 to 0.15625
- down_bias: bfloat16 [1, 384], P(None, ('dp', 'fsdp')), may hold values from -2 to 2
- cotangent: bfloat16 [128, 256, 384], P(('dp', 'fsdp')), may hold values from -6 to 6
Outputs:
- result: bfloat16 [128, 256, 384], P(('dp', 'fsdp'))
- token_grad: float32 [128, 256, 384], P(('dp', 'fsdp'))
- condition_grad: float32 [128, 384], P(('dp', 'fsdp'))
- modulation_weight_grad: float32 [1, 384, 2304], P(None, ('dp', 'fsdp'))
- modulation_bias_grad: float32 [1, 2304], P(None, ('dp', 'fsdp'))
- attend_weight_grad: float32 [1, 384, 1152], P(None, ('dp', 'fsdp'))
- attend_bias_grad: float32 [1, 768], P(None, ('dp', 'fsdp'))
- output_weight_grad: float32 [1, 384, 384], P(None, ('dp', 'fsdp'))
- output_bias_grad: float32 [1, 384], P(None, ('dp', 'fsdp'))
- up_weight_grad: float32 [1, 384, 1536], P(None, ('dp', 'fsdp'))
- up_bias_grad: float32 [1, 1536], P(None, ('dp', 'fsdp'))
- down_weight_grad: float32 [1, 1536, 384], P(None, ('dp', 'fsdp'))
- down_bias_grad: float32 [1, 384], P(None, ('dp', 'fsdp'))
The draws below stay inside these ranges and needn't reach their ends.
All inputs are finite; a program needn't handle non-finite values.
Results may differ from the reference program's by a relative error of at most 0.02.
The reference program's roundings to bfloat16 on the way count: a program that leaves them out, or rounds other values in their place, can miss the bound.
Values may be sent and summed in bfloat16 or wider, within the bound.
A program may use at most 128 MiB of HBM per device.

```python
import jax
import jax.numpy as jnp
from jax import lax

D = 384
HEADS = 6
HEAD = 64
FF = 1536
S = 256
LAYERS = 1
LATENTS = 128


def strengthened(entries, rng, source, target, blocks, factor):
    def block_of(position):
        return (jnp.arange(entries.shape[position]) // (entries.shape[position] // blocks)).reshape((-1,) + (1,) * (entries.ndim - 1 - position))

    near = jax.random.permutation(rng, blocks)[block_of(target)]
    second = (block_of(target) + blocks // 2) % blocks
    return jnp.where((block_of(source) == near) | (block_of(source) == second), factor * entries, entries)


def level_of(stream_key, dims, cuts, least, top_value):
    def one(axis_at, blocks):
        draws = jax.random.uniform(jax.random.fold_in(jax.random.fold_in(stream_key, 6), axis_at), (blocks,), jnp.float32, least / len(cuts), top_value / len(cuts))
        return jnp.repeat(jnp.exp(draws), dims[axis_at] // blocks).reshape((-1,) + (1,) * (len(dims) - axis_at - 1))

    loudness = one(*cuts[0])
    for cut in cuts[1:]:
        loudness = loudness * one(*cut)
    return loudness


def scatter_about(rng, extent, scale, reach, pieces=(), held_as=jnp.bfloat16):
    drawn = jax.random.normal(rng, extent, jnp.float32) * scale
    if len(pieces) > 0:
        drawn = level_of(rng, extent, pieces, -0.22, 0.18) * drawn
    return jnp.clip(drawn, min=-reach, max=reach).astype(held_as)


def gaussian_with(stream_key, shape, deviation, most, pieces, heavy, dtype=jnp.bfloat16):
    drawn = deviation * jax.random.normal(stream_key, shape, jnp.float32)
    if pieces:
        drawn = drawn * level_of(stream_key, shape, pieces, -0.22, 0.18)
    return jnp.clip(strengthened(drawn, jax.random.fold_in(stream_key, 3), *heavy), -most, most).astype(dtype)


def setup_inputs(seed: int = 0) -> dict:
    splits = jax.random.split(jax.random.key(seed), 14)
    return {
        "tokens": gaussian_with(splits[0], (LATENTS, S, D), 1.0, 24.0, ((0, 128),), (0, 2, 128, 5.5)),
        "condition": gaussian_with(splits[1], (LATENTS, D), 1.0, 24.0, ((0, 128),), (0, 1, 128, 5.5)),
        "modulation_weight": scatter_about(splits[2], (LAYERS, D, 6 * D), D ** -0.5, 0.3125, ((1, 128),)),
        "modulation_bias": scatter_about(splits[3], (LAYERS, 6 * D), 0.5, 3.0, ((1, 128),)),
        "attend_weight": scatter_about(splits[4], (LAYERS, D, 3 * D), D ** -0.5, 0.3125, ((1, 128),)),
        "attend_bias": scatter_about(splits[5], (LAYERS, 2 * D), 0.5, 3.0, ((1, 128),)),
        "output_weight": scatter_about(splits[6], (LAYERS, D, D), (D // 16) ** -0.5, 1.25, ((1, 128),)),
        "output_bias": scatter_about(splits[7], (LAYERS, D), 0.3, 2.0, ((1, 128),)),
        "up_weight": scatter_about(splits[8], (LAYERS, D, FF), D ** -0.5, 0.3125, ((1, 128),)),
        "up_bias": scatter_about(splits[9], (LAYERS, FF), 0.5, 3.0, ((1, 128),)),
        "down_weight": scatter_about(splits[10], (LAYERS, FF, D), FF ** -0.5, 0.15625, ((1, 128),)),
        "down_bias": scatter_about(splits[11], (LAYERS, D), 0.3, 2.0, ((1, 128),)),
        "cotangent": scatter_about(splits[12], (LATENTS, S, D), 1.0, 6.0, ((0, 128),)),
    }


@jax.custom_vjp
def low(v):
    return lax.optimization_barrier(v.astype(jnp.bfloat16)).astype(jnp.float32)

@jax.custom_vjp
def low_back(v):
    return v

def low_keep(v):
    return (low(v), None)

def low_pass(kept, grad):
    return (grad,)

def back_keep(v):
    return (v, None)

def back_low(kept, grad):
    return (low(grad),)
low.defvjp(low_keep, low_pass)
low_back.defvjp(back_keep, back_low)
EPS = 1e-06

def precise_dot(left, right):
    return jnp.dot(left, right, precision=lax.Precision.HIGHEST)

def normalize(stream):
    center = lax.optimization_barrier(jnp.mean(stream, axis=-1, keepdims=True))
    shifted = stream - center
    spread = lax.optimization_barrier(jnp.mean(shifted * shifted, axis=-1, keepdims=True))
    return shifted * lax.rsqrt(spread + EPS)

def attention(queries, keys_all, values_all):
    factor = HEAD ** (-0.5)
    raw_scores = jnp.einsum('qhd,khd->hqk', queries, keys_all, precision=lax.Precision.HIGHEST)
    scores = low_back(raw_scores * factor)
    probabilities = jax.nn.softmax(scores, axis=-1)
    return jnp.einsum('hqk,khd->qhd', low(probabilities), values_all, precision=lax.Precision.HIGHEST)

def block(stream, cact_row, w_modulation, b_modulation, w_attend, b_attend, w_output, b_output, w_up, b_up, w_down, b_down):
    model_width = stream.shape[-1]
    token_count = stream.shape[0]
    modulation = precise_dot(cact_row, w_modulation) + b_modulation
    shift_one, scale_one, gate_one, shift_two, scale_two, gate_two = jnp.split(modulation, 6)
    hidden_one = low(normalize(stream) * (1.0 + scale_one) + shift_one)
    zero_keys = jnp.zeros((model_width,), jnp.float32)
    bias_full = jnp.concatenate([b_attend[:model_width], zero_keys, b_attend[model_width:]])
    triple = low_back(precise_dot(hidden_one, w_attend) + bias_full)
    queries = low(triple[:, :model_width]).reshape(token_count, HEADS, HEAD)
    keys_all = low(triple[:, model_width:2 * model_width]).reshape(token_count, HEADS, HEAD)
    values_all = low(triple[:, 2 * model_width:]).reshape(token_count, HEADS, HEAD)
    mixed_heads = low(low_back(attention(queries, keys_all, values_all).reshape(token_count, model_width)))
    branch = low_back(precise_dot(mixed_heads, w_output) + b_output)
    middle = stream + gate_one * branch
    hidden_two = low(normalize(middle) * (1.0 + scale_two) + shift_two)
    upper_in = low_back(precise_dot(hidden_two, w_up) + b_up)
    activated = low(jax.nn.gelu(upper_in, approximate=True))
    feed_out = low_back(precise_dot(activated, w_down) + b_down)
    return middle + gate_two * feed_out

def reference(tokens, condition, modulation_weight, modulation_bias, attend_weight, attend_bias, output_weight, output_bias, up_weight, up_bias, down_weight, down_bias, cotangent):
    weights = (modulation_weight.astype(jnp.float32), modulation_bias.astype(jnp.float32), attend_weight.astype(jnp.float32), attend_bias.astype(jnp.float32), output_weight.astype(jnp.float32), output_bias.astype(jnp.float32), up_weight.astype(jnp.float32), up_bias.astype(jnp.float32), down_weight.astype(jnp.float32), down_bias.astype(jnp.float32))
    group_size = 16

    def forward(stream_all, condition_all, params):
        cact = low(jax.nn.silu(condition_all))

        def run_latent(stream, cact_row):
            for layer_index in range(LAYERS):
                stream = block(stream, cact_row, *[item[layer_index] for item in params])
            return stream

        def group(carry, inputs):
            return (carry, jax.vmap(run_latent)(inputs[0], inputs[1]))
        grouped = (stream_all.reshape(LATENTS // group_size, group_size, S, D), cact.reshape(LATENTS // group_size, group_size, D))
        _, outcome = lax.scan(jax.checkpoint(group), jnp.zeros((), jnp.float32), grouped)
        return outcome.reshape(LATENTS, S, D)
    outcome, pullback = jax.vjp(forward, tokens.astype(jnp.float32), condition.astype(jnp.float32), weights)
    token_grad, condition_grad, weight_grads = pullback(cotangent.astype(jnp.float32))
    return (outcome.astype(jnp.bfloat16), token_grad, condition_grad, weight_grads[0], weight_grads[1], weight_grads[2], weight_grads[3], weight_grads[4], weight_grads[5], weight_grads[6], weight_grads[7], weight_grads[8], weight_grads[9])
```

```python
import functools

import jax
import jax.numpy as jnp
from jax import lax
from jax.experimental import pallas as pl
from jax.experimental.pallas import tpu as pltpu
from jax.sharding import PartitionSpec as P

MESH = pl.DeviceIdType.MESH
F32 = jnp.float32
BF16 = jnp.bfloat16
EPS = 1e-06
HEAD = 64
D = 384
FF = 1536
S = 256
FACTOR = HEAD ** (-0.5)
VMEM_LIMIT = 60 * 1024 * 1024

PARTS = 3
WIDE = 512
ORDERS = ((0, 1, 2), (1, 2, 0), (2, 0, 1))
BIASES = {"mod": (18, 0), "attend": (6, 18), "output": (3, 24), "up": (12, 27), "down": (3, 39)}


def dot(a, b, ca=1, cb=0):
    return lax.dot_general(a, b, (((ca,), (cb,)), ((), ())), preferred_element_type=F32)


def place():
    dp, fsdp = lax.axis_index("dp"), lax.axis_index("fsdp")
    core = lax.rem(dp, 2)
    y = lax.rem(lax.div(dp, 2), 4)
    x = lax.rem(lax.div(dp, 8), 2) + 2 * fsdp
    return (x, y, lax.div(dp, 16)), core


def device(at, core):
    x, y, z = at
    return (z * 16 + lax.rem(x, 2) * 8 + y * 2 + core, lax.div(x, 2))


def moved(at, axis, by):
    return tuple(lax.rem(c + by, 4) if i == axis else c for i, c in enumerate(at))


def slot_of(part, x, y, z, core):
    at = (x, y, z)
    a, b, c = ORDERS[part]
    return ((core * 4 + at[c]) * 4 + at[b]) * 4 + at[a]


def greet(at, core):
    barrier = pltpu.get_barrier_semaphore()
    for axis in range(3):
        for by in range(1, 4):
            pl.semaphore_signal(
                barrier, inc=1, device_id=device(moved(at, axis, by), core), device_id_type=MESH
            )
    pl.semaphore_signal(barrier, inc=1, device_id=device(at, 1 - core), device_id_type=MESH)
    pl.semaphore_wait(barrier, 10)


def remote(src, dst, send, recv, to):
    copy = pltpu.make_async_remote_copy(
        src_ref=src, dst_ref=dst, send_sem=send, recv_sem=recv, device_id=to, device_id_type=MESH
    )
    copy.start()
    return copy


def spread_rows(transposed):
    shape = (256, 256)
    n = lax.broadcasted_iota(jnp.int32, shape, 0 if transposed else 1)
    o = lax.broadcasted_iota(jnp.int32, shape, 1 if transposed else 0)
    member, row = n >> 4, n & 15
    section = (row * 11) >> 5
    target = jnp.where(row == 15, 240 + member, section * 48 + member * 3 + (row - 3 * section))
    return jnp.where(target == o, 1.0, 0.0).astype(BF16)


def spread_down(transposed):
    shape = (256, 192) if transposed else (192, 256)
    n = lax.broadcasted_iota(jnp.int32, shape, 0 if transposed else 1)
    o = lax.broadcasted_iota(jnp.int32, shape, 1 if transposed else 0)
    member, row = n >> 4, n & 15
    target = jnp.where(row < 12, member * 12 + row, -1)
    return jnp.where(target == o, 1.0, 0.0).astype(BF16)


def members(part, group):
    z, x_lo = group // 2, group % 2
    return [
        slot_of(part, 2 * x_hi + x_lo, y, z, core)
        for y in range(4)
        for core in range(2)
        for x_hi in range(2)
    ]


def gather_kernel(
    mod, b_mod, att, b_att, out, b_out, up, b_up, down, b_down,
    w_mod, w_att, w_out, w_up, w_down, bias,
    held, send1, recv1, send2, recv2, send3, recv3, send4, recv4, send_c, recv_c,
):
    at, core = place()

    def load(ref, lo, hi):
        return ref[0, :, lo:hi].astype(F32)

    row = jnp.concatenate(
        [ref[...].astype(F32) for ref in (b_mod, b_att, b_out, b_up, b_down)]
        + [jnp.zeros((1, 1152 - 42), F32)],
        axis=1,
    )
    main = jnp.concatenate(
        [
            load(mod, 0, 1152),
            load(mod, 1152, 2304),
            load(att, 0, 1152),
            load(up, 0, 1152),
            jnp.concatenate([load(up, 1152, 1536), load(out, 0, 384), jnp.zeros((3, 384), F32)], axis=1),
            row,
        ],
        axis=0,
    ).astype(BF16)
    rest = jnp.concatenate([load(down, 0, 384), jnp.zeros((4, 384), F32)], axis=0).astype(BF16)
    own = [slot_of(p, *at, core) for p in range(PARTS)]
    held[0, own[0]] = main[:, 0:512]
    held[1, own[1]] = main[:, 512:1024]
    held[2, own[2], :, 0:128] = main[:, 1024:1152]
    held[2, own[2], :, 128:512] = rest

    greet(at, core)
    copies = []

    def first(p):
        block = held.at[p, pl.ds(own[p], 1)]
        return [
            remote(block, block, send1.at[p, d - 1], recv1.at[p, d - 1], device(moved(at, ORDERS[p][0], d), core))
            for d in (1, 3, 2)
        ]

    def second(p):
        _, b, c = ORDERS[p]
        block = held.at[p, pl.ds(((core * 4 + at[c]) * 4 + at[b]) * 4, 4)]
        return [
            remote(block, block, send2.at[p, d - 1], recv2.at[p, d - 1], device(moved(at, b, d), core))
            for d in (1, 3, 2)
        ]

    def plane(p, by, lo=0, count=16):
        c = ORDERS[p][2]
        return held.at[p, pl.ds((core * 4 + lax.rem(at[c] + by, 4)) * 16 + lo, count)]

    def across(p, k, block):
        return remote(block, block, send_c.at[p, k], recv_c.at[p, k], device(at, 1 - core))

    stage1 = [first(p) for p in range(PARTS)]
    stage2 = []
    for p in range(PARTS):
        for copy in stage1[p]:
            copy.wait_recv()
        stage2.append(second(p))
    stage3 = []
    for p in range(PARTS):
        for copy in stage2[p]:
            copy.wait_recv()
        c = ORDERS[p][2]
        block = plane(p, 0)
        stage3.append(
            [
                remote(block, block, send3.at[p, k], recv3.at[p, k], device(moved(at, c, by), core))
                for k, by in enumerate((1, 3))
            ]
        )
        copies.append(across(p, 0, block))
    stage4 = []
    for p in range(PARTS):
        c = ORDERS[p][2]
        for k, by in enumerate((3, 1)):
            stage3[p][k].wait_recv()
            half = plane(p, by, 8 * k, 8)
            stage4.append(
                remote(half, half, send4.at[p, k], recv4.at[p, k], device(moved(at, c, 4 - by), core))
            )
            copies.append(across(p, 1 + k, plane(p, by)))
    for p in range(PARTS):
        for k in range(2):
            stage4[2 * p + k].wait_recv()
            copies.append(across(p, 3 + k, plane(p, 2, 8 * k, 8)))
    for copy in copies:
        copy.wait_recv()
    for copy in sum(stage1 + stage2 + stage3, []) + stage4 + copies:
        copy.wait_send()

    rows, rows_down = spread_rows(False), spread_down(False)
    for group in range(8):
        at48, at192, at16 = 48 * group, 192 * group, 16 * group
        for p in range(PARTS):
            blocks = jnp.concatenate([held[p, s] for s in members(p, group)], axis=0)
            wide = WIDE if p < 2 else 128
            laid = dot(rows, blocks[:, :wide]).astype(BF16)
            lo = WIDE * p
            here = slice(at48, at48 + 48)
            w_mod[here, lo : lo + wide] = laid[0:48]
            w_mod[here, 1152 + lo : 1152 + lo + wide] = laid[48:96]
            w_att[here, lo : lo + wide] = laid[96:144]
            w_up[here, lo : lo + wide] = laid[144:192]
            if p == 0:
                w_up[here, 1152:1536] = laid[192:240, 0:384]
                w_out[here, 0:128] = laid[192:240, 384:512]
                bias[at16 : at16 + 16, :] = laid[240:256, 0:128]
            if p == 1:
                w_out[here, 128:384] = laid[192:240, 0:256]
            if p == 2:
                w_down[at192 : at192 + 192, :] = dot(rows_down, blocks[:, 128:512]).astype(BF16)


def bias_map(name, count):
    size, lane = BIASES[name]
    n = lax.broadcasted_iota(jnp.int32, (128, count), 1)
    owner = (n * -(-65536 // size)) >> 16
    k = lax.broadcasted_iota(jnp.int32, (128, count), 0)
    return owner == k, (n - owner * size + lane) == k


def bias_row(bias, name, count):
    mine, lane = bias_map(name, count)
    picked = dot(bias, jnp.where(lane, 1.0, 0.0).astype(BF16))
    return jnp.sum(jnp.where(mine, picked, 0.0), axis=0, keepdims=True)


def bias_block(row, name):
    mine, lane = bias_map(name, row.shape[1])
    placed = jnp.where(mine, row, 0.0).astype(BF16)
    return dot(placed, jnp.where(lane, 1.0, 0.0).astype(BF16), 1, 1)


def normalize(v):
    shifted = v - jnp.mean(v, axis=-1, keepdims=True)
    inverse = lax.rsqrt(jnp.mean(shifted * shifted, axis=-1, keepdims=True) + EPS)
    return shifted * inverse, inverse


def denormalize(e, n, inverse):
    return inverse * (
        e - jnp.mean(e, axis=-1, keepdims=True) - n * jnp.mean(e * n, axis=-1, keepdims=True)
    )


def total(v):
    return jnp.sum(v, axis=0, keepdims=True)


def block_kernel(
    tokens, condition, cotangent, w_mod, w_att, w_out, w_up, w_down, bias,
    result, token_grad, condition_grad, packed,
    d_mod, d_att, d_out, d_up, d_down, probs_ref,
):
    x = tokens[0].astype(F32)
    g = cotangent[0].astype(F32)
    cond = condition[...].astype(F32)
    sigmoid = 1.0 / (1.0 + jnp.exp(-cond))
    cact = (cond * sigmoid).astype(BF16).astype(F32)
    cact_column = jnp.broadcast_to(cact, (128, D)).T
    raw_bias = bias[...]
    modulation = jnp.concatenate(
        [total(w_mod[:, 128 * t : 128 * t + 128].astype(F32) * cact_column) for t in range(18)],
        axis=1,
    ) + bias_row(raw_bias, "mod", 6 * D)
    shift1, scale1, gate1, shift2, scale2, gate2 = [
        modulation[:, D * i : D * i + D] for i in range(6)
    ]
    n1, inverse1 = normalize(x)
    hidden1 = (n1 * (1.0 + scale1) + shift1).astype(BF16)
    b_att = bias_row(raw_bias, "attend", 2 * D)
    b_full = jnp.concatenate([b_att[:, :D], jnp.zeros((1, D), F32), b_att[:, D:]], axis=1)
    triple = (dot(hidden1, w_att[...]) + b_full).astype(BF16)

    def pair(i, which):
        lo = D * which + 128 * i
        return triple[:, lo : lo + 128]

    lane = lax.broadcasted_iota(jnp.int32, (S, 128), 1)
    halves = [lane < 64, lane >= 64]
    nothing = jnp.zeros((S, 128), BF16)
    mixed_pairs = []
    keys_t = []
    for i in range(3):
        q, k, v = pair(i, 0), pair(i, 1), pair(i, 2)
        v_t = v.T
        keys_t.append(k.T)
        mixed_t = []
        for h in range(2):
            scores = dot(k, jnp.where(halves[h], q, nothing), 1, 1) * FACTOR
            e = jnp.exp(scores - jnp.max(scores, axis=0, keepdims=True))
            probs = e * (1.0 / total(e))
            probs_ref[2 * i + h] = probs
            mixed_t.append(dot(v_t[64 * h : 64 * h + 64], probs.astype(BF16)))
        mixed_pairs.append(jnp.concatenate(mixed_t, axis=0).T.astype(BF16))
    mixed = jnp.concatenate(mixed_pairs, axis=1)
    branch = dot(mixed, w_out[...]) + bias_row(raw_bias, "output", D)
    middle = x + gate1 * branch
    n2, inverse2 = normalize(middle)
    hidden2 = (n2 * (1.0 + scale2) + shift2).astype(BF16)

    b_up = bias_row(raw_bias, "up", FF)
    dfeed = (gate2 * g).astype(BF16)
    feed = jnp.zeros((S, D), F32)
    dhidden2 = jnp.zeros((S, D), F32)
    db_up = []
    hidden2_t = hidden2.T
    for c in range(4):
        lo = D * c
        upper = dot(hidden2, w_up[:, lo : lo + D]) + b_up[:, lo : lo + D]
        square = upper * upper
        t = jnp.tanh(0.7978845608028654 * (upper + 0.044715 * (upper * square)))
        half = 0.5 * (1.0 + t)
        activated = (upper * half).astype(BF16)
        slope = half + (0.5 * upper) * (1.0 - t * t) * (
            0.7978845608028654 * (1.0 + 0.134145 * square)
        )
        feed = feed + dot(activated, w_down[lo : lo + D, :])
        dupper = (dot(dfeed, w_down[lo : lo + D, :], 1, 1) * slope).astype(BF16)
        d_down[lo : lo + D, :] = dot(activated.T, dfeed).astype(BF16)
        d_up[:, lo : lo + D] = dot(hidden2_t, dupper).astype(BF16)
        db_up.append(total(dupper.astype(F32)))
        dhidden2 = dhidden2 + dot(dupper, w_up[:, lo : lo + D], 1, 1)
    feed = feed + bias_row(raw_bias, "down", D)
    result[0] = (middle + gate2 * feed).astype(BF16)
    dgate2 = total(g * feed)
    db_down = total(dfeed.astype(F32))
    dscale2, dshift2 = total(dhidden2 * n2), total(dhidden2)
    gmid = g + denormalize(dhidden2 * (1.0 + scale2), n2, inverse2)
    dgate1 = total(gmid * branch)
    dbranch = (gate1 * gmid).astype(BF16)
    d_out[...] = dot(mixed.T, dbranch).astype(BF16)
    db_out = total(dbranch.astype(F32))
    dmixed = dot(dbranch, w_out[...], 1, 1).astype(BF16)

    dq, dk, dv = [], [], []
    for i in range(3):
        q, v = pair(i, 0), pair(i, 2)
        dm = dmixed[:, 128 * i : 128 * i + 128]
        dq_t, dk_h, dv_h = [], [], []
        for h in range(2):
            probs = probs_ref[2 * i + h]
            dprobs = dot(v, jnp.where(halves[h], dm, nothing), 1, 1)
            dv_h.append(dot(probs.astype(BF16), dm))
            dscores = (probs * (dprobs - total(probs * dprobs))).astype(BF16)
            dk_h.append(dot(dscores, q))
            dq_t.append(dot(keys_t[i][64 * h : 64 * h + 64], dscores))
        dq.append((jnp.concatenate(dq_t, axis=0).T * FACTOR).astype(BF16))
        dk.append((jnp.where(halves[0], dk_h[0], dk_h[1]) * FACTOR).astype(BF16))
        dv.append(jnp.where(halves[0], dv_h[0], dv_h[1]).astype(BF16))
    dtriple = jnp.concatenate(dq + dk + dv, axis=1)
    d_att[...] = dot(hidden1.T, dtriple).astype(BF16)
    sums = total(dtriple.astype(F32))
    db_att = jnp.concatenate([sums[:, :D], sums[:, 2 * D :]], axis=1)
    dhidden1 = dot(dtriple, w_att[...], 1, 1)
    dscale1, dshift1 = total(dhidden1 * n1), total(dhidden1)
    token_grad[0] = gmid + denormalize(dhidden1 * (1.0 + scale1), n1, inverse1)

    dmod = jnp.concatenate([dshift1, dscale1, dgate1, dshift2, dscale2, dgate2], axis=1)
    dcact = jnp.zeros((D, 128), F32)
    for t in range(18):
        here = slice(128 * t, 128 * t + 128)
        dcact = dcact + w_mod[:, here].astype(F32) * dmod[:, here]
        d_mod[:, here] = (cact_column * dmod[:, here]).astype(BF16)
    condition_grad[...] = total(dcact.T) * (sigmoid * (1.0 + cond * (1.0 - sigmoid)))

    d_bias = (
        bias_block(dmod, "mod")
        + bias_block(db_att, "attend")
        + bias_block(db_out, "output")
        + bias_block(jnp.concatenate(db_up, axis=1), "up")
        + bias_block(db_down, "down")
    ).astype(BF16)
    rows, rows_down = spread_rows(True), spread_down(True)
    for group in range(8):
        here = slice(48 * group, 48 * group + 48)
        for p in range(PARTS):
            wide = WIDE if p < 2 else 128
            lo = WIDE * p
            if p == 0:
                mix = jnp.concatenate([d_up[here, 1152:1536], d_out[here, 0:128]], axis=1)
                last = jnp.concatenate(
                    [d_bias[16 * group : 16 * group + 16], jnp.zeros((16, 384), BF16)], axis=1
                )
            elif p == 1:
                mix = jnp.concatenate([d_out[here, 128:384], jnp.zeros((48, 256), BF16)], axis=1)
                last = jnp.zeros((16, wide), BF16)
            else:
                mix = jnp.zeros((48, wide), BF16)
                last = jnp.zeros((16, wide), BF16)
            laid = dot(
                rows,
                jnp.concatenate(
                    [
                        d_mod[here, lo : lo + wide],
                        d_mod[here, 1152 + lo : 1152 + lo + wide],
                        d_att[here, lo : lo + wide],
                        d_up[here, lo : lo + wide],
                        mix,
                        last,
                    ],
                    axis=0,
                ),
            ).astype(BF16)
            for m, s in enumerate(members(p, group)):
                packed[p, s, :, 0:wide] = laid[16 * m : 16 * m + 16]
            if p == 2:
                laid = dot(rows_down, d_down[192 * group : 192 * group + 192, :]).astype(BF16)
                for m, s in enumerate(members(p, group)):
                    packed[p, s, :, 128:512] = laid[16 * m : 16 * m + 16]


def reduce_kernel(
    packed, final,
    chip, ours, pass_on, turned, joined, ring, row, near, line, ends,
    send_c, recv_c, send1, recv1, send2, recv2, send3, recv3, send4, recv4,
):
    at, core = place()
    greet(at, core)

    def add(*blocks):
        out = blocks[0].astype(F32)
        for block in blocks[1:]:
            out = out + block.astype(F32)
        return out

    def chunk(p, by):
        return lax.rem(at[ORDERS[p][2]] + by, 4) * 16

    cross = {}
    for by in (2, 1, 3, 0):
        for p in range(PARTS):
            lo = chunk(p, by)
            cross[p, by] = remote(
                packed.at[p, pl.ds((1 - core) * 64 + lo, 16)],
                chip.at[p, pl.ds(lo, 16)],
                send_c.at[p, by],
                recv_c.at[p, by],
                device(at, 1 - core),
            )

    def to(p, by):
        return device(moved(at, ORDERS[p][2], by), core)

    waits = []
    for by in (2, 1, 3, 0):
        for p in range(PARTS):
            lo = chunk(p, by)
            cross[p, by].wait_recv()
            here = pl.ds(lo, 16)
            ours[p, here] = add(packed[p, pl.ds(core * 64 + lo, 16)], chip[p, here]).astype(BF16)
            if by == 2:
                for k in range(2):
                    waits.append(
                        remote(ours.at[p, pl.ds(lo + 8 * k, 8)], pass_on.at[p, k], send1.at[p, k], recv1.at[p, k], to(p, (1, 3)[k]))
                    )
            if by in (1, 3):
                k = (1, 3).index(by)
                waits.append(
                    remote(ours.at[p, pl.ds(lo + 8 * (1 - k), 8)], ring.at[p, k, pl.ds(8 * (1 - k), 8)], send1.at[p, 2 + k], recv1.at[p, 2 + k], to(p, by))
                )
    for p in range(PARTS):
        for k in range(2):
            waits[2 * p + k].wait_recv()
            lo = chunk(p, (1, 3)[k]) + 8 * k
            turned[p, k] = add(ours[p, pl.ds(lo, 8)], pass_on[p, k]).astype(BF16)
            waits.append(
                remote(turned.at[p, k], ring.at[p, k, pl.ds(8 * k, 8)], send2.at[p, k], recv2.at[p, k], to(p, (1, 3)[k]))
            )
    for p in range(PARTS):
        for k in range(2):
            waits[6 + 3 * k + p].wait_recv()
            waits[12 + 2 * p + k].wait_recv()
        joined[p] = add(ours[p, pl.ds(chunk(p, 0), 16)], ring[p, 0], ring[p, 1]).astype(BF16)
        b = ORDERS[p][1]
        for d in (2, 1, 3):
            waits.append(
                remote(joined.at[p, pl.ds(lax.rem(at[b] + d, 4) * 4, 4)], row.at[p, d - 1], send3.at[p, d - 1], recv3.at[p, d - 1], device(moved(at, b, d), core))
            )
    for p in range(PARTS):
        a, b, _ = ORDERS[p]
        for d in range(3):
            waits[18 + 3 * p + d].wait_recv()
        near[p] = add(joined[p, pl.ds(at[b] * 4, 4)], row[p, 0], row[p, 1], row[p, 2])
        line[p] = near[p].astype(BF16)
        for d in (2, 1, 3):
            waits.append(
                remote(line.at[p, pl.ds(lax.rem(at[a] + d, 4), 1)], ends.at[p, pl.ds(d - 1, 1)], send4.at[p, d - 1], recv4.at[p, d - 1], device(moved(at, a, d), core))
            )
    for p in range(PARTS):
        for d in range(3):
            waits[27 + 3 * p + d].wait_recv()
        final[:, WIDE * p : WIDE * p + WIDE] = add(near[p, at[ORDERS[p][0]]], ends[p, 0], ends[p, 1], ends[p, 2])
    for copy in [*cross.values(), *waits]:
        copy.wait_send()


def unpack_kernel(block, mod, b_mod, att, b_att, out, b_out, up, b_up, down, b_down):
    mod[0, :, 0:1152] = block[0:3, 0:1152]
    mod[0, :, 1152:2304] = block[3:6, 0:1152]
    att[0] = block[6:9, 0:1152]
    up[0, :, 0:1152] = block[9:12, 0:1152]
    up[0, :, 1152:1536] = block[12:15, 0:384]
    out[0] = block[12:15, 384:768]
    down[0] = block[0:12, 1152:1536]
    for ref, name in ((b_mod, "mod"), (b_att, "attend"), (b_out, "output"), (b_up, "up"), (b_down, "down")):
        size, lane = BIASES[name]
        ref[...] = block[15:16, lane : lane + size]


def whole(count):
    return [pl.BlockSpec(memory_space=pltpu.VMEM)] * count


def shape(*dims, dtype=BF16):
    return jax.ShapeDtypeStruct(dims, dtype)


def dma(*dims):
    return pltpu.SemaphoreType.DMA(dims)


def local(
    tokens, condition, modulation_weight, modulation_bias, attend_weight, attend_bias, output_weight, output_bias,
    up_weight, up_bias, down_weight, down_bias, cotangent,
):
    gathered = pl.pallas_call(
        gather_kernel,
        out_shape=[
            shape(D, 6 * D), shape(D, 3 * D), shape(D, D), shape(D, FF), shape(FF, D), shape(128, 128),
        ],
        in_specs=whole(10),
        out_specs=whole(6),
        scratch_shapes=[
            pltpu.VMEM((PARTS, 128, 16, WIDE), BF16),
            dma(PARTS, 3), dma(PARTS, 3), dma(PARTS, 3), dma(PARTS, 3), dma(PARTS, 2), dma(PARTS, 2),
            dma(PARTS, 2), dma(PARTS, 2), dma(PARTS, 5), dma(PARTS, 5),
        ],
        compiler_params=pltpu.CompilerParams(
            collective_id=0, has_side_effects=True, vmem_limit_bytes=VMEM_LIMIT
        ),
    )(
        modulation_weight, modulation_bias, attend_weight, attend_bias, output_weight, output_bias,
        up_weight, up_bias, down_weight, down_bias,
    )
    result, token_grad, condition_grad, packed = pl.pallas_call(
        block_kernel,
        out_shape=[
            shape(1, S, D), shape(1, S, D, dtype=F32), shape(1, D, dtype=F32), shape(PARTS, 128, 16, WIDE),
        ],
        in_specs=whole(9),
        out_specs=whole(4),
        scratch_shapes=[
            pltpu.VMEM((D, 6 * D), BF16), pltpu.VMEM((D, 3 * D), BF16), pltpu.VMEM((D, D), BF16),
            pltpu.VMEM((D, FF), BF16), pltpu.VMEM((FF, D), BF16), pltpu.VMEM((6, S, S), F32),
        ],
        compiler_params=pltpu.CompilerParams(vmem_limit_bytes=VMEM_LIMIT),
    )(tokens, condition, cotangent, *gathered)
    final = pl.pallas_call(
        reduce_kernel,
        out_shape=shape(16, 3 * WIDE, dtype=F32),
        in_specs=whole(1),
        out_specs=pl.BlockSpec(memory_space=pltpu.VMEM),
        scratch_shapes=[
            pltpu.VMEM((PARTS, 64, 16, WIDE), BF16),
            pltpu.VMEM((PARTS, 64, 16, WIDE), BF16),
            pltpu.VMEM((PARTS, 2, 8, 16, WIDE), BF16),
            pltpu.VMEM((PARTS, 2, 8, 16, WIDE), BF16),
            pltpu.VMEM((PARTS, 16, 16, WIDE), BF16),
            pltpu.VMEM((PARTS, 2, 16, 16, WIDE), BF16),
            pltpu.VMEM((PARTS, 3, 4, 16, WIDE), BF16),
            pltpu.VMEM((PARTS, 4, 16, WIDE), F32),
            pltpu.VMEM((PARTS, 4, 16, WIDE), BF16),
            pltpu.VMEM((PARTS, 3, 16, WIDE), BF16),
            dma(PARTS, 4), dma(PARTS, 4), dma(PARTS, 4), dma(PARTS, 4), dma(PARTS, 2), dma(PARTS, 2),
            dma(PARTS, 3), dma(PARTS, 3), dma(PARTS, 3), dma(PARTS, 3),
        ],
        compiler_params=pltpu.CompilerParams(
            collective_id=1, has_side_effects=True, vmem_limit_bytes=VMEM_LIMIT
        ),
    )(packed)
    grads = pl.pallas_call(
        unpack_kernel,
        out_shape=[
            shape(1, 3, 6 * D, dtype=F32), shape(1, 18, dtype=F32), shape(1, 3, 3 * D, dtype=F32),
            shape(1, 6, dtype=F32), shape(1, 3, D, dtype=F32), shape(1, 3, dtype=F32),
            shape(1, 3, FF, dtype=F32), shape(1, 12, dtype=F32), shape(1, 12, D, dtype=F32), shape(1, 3, dtype=F32),
        ],
        in_specs=whole(1),
        out_specs=whole(10),
    )(final)
    return (result, token_grad, condition_grad, *grads)


def solution(mesh):
    latents = P(("dp", "fsdp"), None, None)
    rows = P(None, ("dp", "fsdp"), None)
    entries = P(None, ("dp", "fsdp"))
    weights = (rows, entries) * 5
    return jax.shard_map(
        local,
        mesh=mesh,
        in_specs=(latents, P(("dp", "fsdp"), None), *weights, latents),
        out_specs=(latents, latents, P(("dp", "fsdp"), None), *weights),
        check_vma=False,
    )
```

```python
import jax
import jax.numpy as jnp
from jax import lax
from jax.experimental import pallas as pl
from jax.experimental.pallas import tpu as pltpu
from jax.sharding import PartitionSpec as P

MESH = pl.DeviceIdType.MESH
F32 = jnp.float32
BF16 = jnp.bfloat16
EPS = 1e-06
HEAD = 64
D = 384
FF = 1536
S = 256
FACTOR = HEAD ** (-0.5)
VMEM_LIMIT = 60 * 1024 * 1024

PARTS = 3
ORDERS = ((0, 1, 2), (1, 2, 0), (2, 0, 1))
BIASES = {"mod": (18, 0, 0), "attend": (6, 18, 0), "output": (3, 24, 6), "up": (12, 27, 9), "down": (3, 39, 21)}


def dot(a, b, ca=1, cb=0):
    return lax.dot_general(a, b, (((ca,), (cb,)), ((), ())), preferred_element_type=F32)


def place():
    dp, fsdp = lax.axis_index("dp"), lax.axis_index("fsdp")
    core = lax.rem(dp, 2)
    y = lax.rem(lax.div(dp, 2), 4)
    x = lax.rem(lax.div(dp, 8), 2) + 2 * fsdp
    return (x, y, lax.div(dp, 16)), core


def device(at, core):
    x, y, z = at
    return (z * 16 + lax.rem(x, 2) * 8 + y * 2 + core, lax.div(x, 2))


def moved(at, axis, by):
    return tuple(lax.rem(c + by, 4) if i == axis else c for i, c in enumerate(at))


def slot_of(part, x, y, z, core):
    at = (x, y, z)
    a, b, c = ORDERS[part]
    return ((core * 4 + at[c]) * 4 + at[b]) * 4 + at[a]


def announce(at, core):
    barrier = pltpu.get_barrier_semaphore()
    for axis in range(3):
        for by in range(1, 4):
            pl.semaphore_signal(
                barrier, inc=1, device_id=device(moved(at, axis, by), core), device_id_type=MESH
            )
    pl.semaphore_signal(barrier, inc=1, device_id=device(at, 1 - core), device_id_type=MESH)


class Moves:
    def __init__(self, at, core, send, recv):
        self.at, self.core, self.send, self.recv = at, core, send, recv
        self.copies = {}

    def start(self, stage, p, k, src, dst, axis, by):
        to = device(self.at, 1 - self.core) if axis is None else device(moved(self.at, axis, by), self.core)
        copy = pltpu.make_async_remote_copy(
            src_ref=src, dst_ref=dst, send_sem=self.send.at[stage, p, k], recv_sem=self.recv.at[stage, p, k],
            device_id=to, device_id_type=MESH,
        )
        copy.start()
        self.copies[stage, p, k] = copy

    def arrived(self, stage, p, ks):
        for k in ks:
            self.copies[stage, p, k].wait_recv()

    def sent(self):
        for copy in self.copies.values():
            copy.wait_send()


class Gather(Moves):
    def __init__(self, at, core, held, send, recv):
        super().__init__(at, core, send, recv)
        self.held = held

    def own(self, p):
        return slot_of(p, *self.at, self.core)

    def first(self, p):
        block = self.held.at[p, pl.ds(self.own(p), 1)]
        for d in (1, 3, 2):
            self.start(0, p, d, block, block, ORDERS[p][0], d)

    def second(self, p):
        self.arrived(0, p, (1, 3, 2))
        _, b, c = ORDERS[p]
        block = self.held.at[p, pl.ds(((self.core * 4 + self.at[c]) * 4 + self.at[b]) * 4, 4)]
        for d in (1, 3, 2):
            self.start(1, p, d, block, block, b, d)

    def plane(self, p, by):
        lo = (self.core * 4 + lax.rem(self.at[ORDERS[p][2]] + by, 4)) * 16
        return self.held.at[p, pl.ds(lo, 16)]

    def third(self, p):
        self.arrived(1, p, (1, 3, 2))
        block = self.plane(p, 0)
        for d in (1, 3, 2):
            self.start(2, p, d, block, block, ORDERS[p][2], d)
        self.start(3, p, 0, block, block, None, 0)

    def across(self, p, d):
        self.arrived(2, p, (d,))
        block = self.plane(p, 4 - d)
        self.start(3, p, d, block, block, None, 0)

    def complete(self, p):
        self.arrived(3, p, range(4))


def add(*blocks):
    out = blocks[0].astype(F32)
    for block in blocks[1:]:
        out = out + block.astype(F32)
    return out


class Reduce(Moves):
    def __init__(self, at, core, packed, chip, ours, ring, joined, row, near, line, ends, send, recv):
        super().__init__(at, core, send, recv)
        self.packed, self.chip, self.ours, self.ring, self.joined = packed, chip, ours, ring, joined
        self.row, self.near, self.line, self.ends = row, near, line, ends

    def chunk(self, p, by):
        return lax.rem(self.at[ORDERS[p][2]] + by, 4) * 16

    def across(self, p):
        for by in (2, 1, 3, 0):
            lo = self.chunk(p, by)
            src = self.packed.at[p, pl.ds((1 - self.core) * 64 + lo, 16)]
            self.start(0, p, by, src, self.chip.at[p, pl.ds(lo, 16)], None, 0)

    def third(self, p):
        for by in (2, 1, 3, 0):
            lo = self.chunk(p, by)
            here = pl.ds(lo, 16)
            self.arrived(0, p, (by,))
            self.ours[p, here] = add(self.packed[p, pl.ds(self.core * 64 + lo, 16)], self.chip[p, here]).astype(BF16)
            if by:
                self.start(1, p, by, self.ours.at[p, here], self.ring.at[p, by - 1], ORDERS[p][2], by)

    def second(self, p):
        self.arrived(1, p, (1, 3, 2))
        ring = self.ring
        self.joined[p] = add(self.ours[p, pl.ds(self.chunk(p, 0), 16)], ring[p, 0], ring[p, 1], ring[p, 2]).astype(BF16)
        b = ORDERS[p][1]
        for d in (2, 1, 3):
            src = self.joined.at[p, pl.ds(lax.rem(self.at[b] + d, 4) * 4, 4)]
            self.start(2, p, d, src, self.row.at[p, d - 1], b, d)

    def first(self, p):
        self.arrived(2, p, (1, 3, 2))
        a, b, _ = ORDERS[p]
        row = self.row
        self.near[p] = add(self.joined[p, pl.ds(self.at[b] * 4, 4)], row[p, 0], row[p, 1], row[p, 2])
        self.line[p] = self.near[p].astype(BF16)
        for d in (2, 1, 3):
            src = self.line.at[p, pl.ds(lax.rem(self.at[a] + d, 4), 1)]
            self.start(3, p, d, src, self.ends.at[p, pl.ds(d - 1, 1)], a, d)

    def total(self, p):
        self.arrived(3, p, (1, 3, 2))
        ends = self.ends
        return add(self.near[p, self.at[ORDERS[p][0]]], ends[p, 0], ends[p, 1], ends[p, 2])


def spread(place_of, count, transposed):
    shape = (256, count) if transposed else (count, 256)
    n = lax.broadcasted_iota(jnp.int32, shape, 0 if transposed else 1)
    o = lax.broadcasted_iota(jnp.int32, shape, 1 if transposed else 0)
    return jnp.where(place_of(n >> 4, n & 15) == o, 1.0, 0.0).astype(BF16)


def threes(member, row):
    section = (row * 11) >> 5
    return section * 48 + member * 3 + (row - 3 * section)


def place_first(member, row):
    return jnp.where(row == 15, 240 + member, threes(member, row))


def place_up(member, row):
    return jnp.where(row < 6, threes(member, row), -1)


def place_left(member, row):
    return jnp.where((row >= 6) & (row < 12), member * 12 + row - 6, -1)


def place_right(member, row):
    return jnp.where((row >= 6) & (row < 12), member * 12 + row, -1)


def place_back(member, row):
    return jnp.where(row < 6, threes(member, row), jnp.where((row >= 12) & (row < 15), threes(member, row) - 96, -1))


def place_attend(member, row):
    return jnp.where(row < 9, threes(member, row), jnp.where(row == 9, 144 + member, -1))


def members(part, group):
    z, x_lo = group // 2, group % 2
    return [
        slot_of(part, 2 * x_hi + x_lo, y, z, core)
        for y in range(4)
        for core in range(2)
        for x_hi in range(2)
    ]


def bias_map(name, count, lane):
    size = BIASES[name][0]
    n = lax.broadcasted_iota(jnp.int32, (128, count), 1)
    owner = (n * -(-65536 // size)) >> 16
    k = lax.broadcasted_iota(jnp.int32, (128, count), 0)
    return owner == k, (n - owner * size + lane) == k


def bias_row(bias, name, count):
    mine, lane = bias_map(name, count, BIASES[name][1])
    picked = dot(bias, jnp.where(lane, 1.0, 0.0).astype(BF16))
    return jnp.sum(jnp.where(mine, picked, 0.0), axis=0, keepdims=True)


def bias_block(row, name):
    mine, lane = bias_map(name, row.shape[1], BIASES[name][2])
    placed = jnp.where(mine, row, 0.0).astype(BF16)
    return dot(placed, jnp.where(lane, 1.0, 0.0).astype(BF16), 1, 1)


def normalize(v):
    shifted = v - jnp.mean(v, axis=-1, keepdims=True)
    inverse = lax.rsqrt(jnp.mean(shifted * shifted, axis=-1, keepdims=True) + EPS)
    return shifted * inverse, inverse


def denormalize(e, n, inverse):
    return inverse * (
        e - jnp.mean(e, axis=-1, keepdims=True) - n * jnp.mean(e * n, axis=-1, keepdims=True)
    )


def total(v):
    return jnp.sum(v, axis=0, keepdims=True)


def block_kernel(
    tokens, condition, mod, b_mod, att, b_att, out, b_out, up, b_up, down, b_down, cotangent,
    result, token_grad, condition_grad, grad_ff, grad_att, grad_mod,
    held1, held2, held3, w_mod, w_att, w_out, w_up, w_down, bias, cact_all,
    d_att, d_out, d_up, d_down, probs_ref,
    packed, chip, ours, ring, joined, row, near, line, ends,
    packed_a, chip_a, ours_a, ring_a, joined_a, row_a, near_a, line_a, ends_a,
    sems,
):
    at, core = place()
    announce(at, core)
    first, second, third = [
        Gather(at, core, held, sems.at[i, 0], sems.at[i, 1]) for i, held in enumerate((held1, held2, held3))
    ]
    back = Reduce(at, core, packed, chip, ours, ring, joined, row, near, line, ends, sems.at[3, 0], sems.at[3, 1])
    last = Reduce(
        at, core, packed_a, chip_a, ours_a, ring_a, joined_a, row_a, near_a, line_a, ends_a, sems.at[4, 0], sems.at[4, 1]
    )

    def load(ref, lo, hi):
        return ref[0, :, lo:hi].astype(F32)

    cond = condition[...].astype(F32)
    sigmoid = 1.0 / (1.0 + jnp.exp(-cond))
    cact = (cond * sigmoid).astype(BF16).astype(F32)
    bias_line = jnp.concatenate(
        [ref[...].astype(F32) for ref in (b_mod, b_att, b_out, b_up, b_down)]
        + [jnp.zeros((1, 128 - 42), F32), cact, jnp.zeros((1, 256), F32)],
        axis=1,
    )
    mine = jnp.concatenate(
        [load(mod, 0, 768), load(mod, 768, 1536), load(mod, 1536, 2304), load(att, 0, 768),
         jnp.concatenate([load(att, 768, 1152), load(out, 0, 384)], axis=1), bias_line],
        axis=0,
    ).astype(BF16)
    tall = down[0].astype(F32)
    mine2 = jnp.concatenate(
        [load(up, 0, 768), load(up, 768, 1536), jnp.concatenate([tall[0:6], tall[6:12]], axis=1), jnp.zeros((4, 768), F32)],
        axis=0,
    ).astype(BF16)
    for p in range(PARTS):
        held1[p, first.own(p)] = mine[:, 256 * p : 256 * p + 256]
        held2[p, second.own(p)] = mine2[:, 256 * p : 256 * p + 256]

    pl.semaphore_wait(pltpu.get_barrier_semaphore(), 10)
    for p in range(PARTS):
        first.first(p)
    for p in range(PARTS):
        second.first(p)

    x = tokens[0].astype(F32)
    g = cotangent[0].astype(F32)
    cact_column = jnp.broadcast_to(cact, (128, D)).T
    n1, inverse1 = normalize(x)

    for p in range(PARTS):
        first.second(p)
    for p in range(PARTS):
        second.second(p)
    for p in range(PARTS):
        first.third(p)
    for p in range(PARTS):
        second.third(p)
    for d in (1, 3, 2):
        for p in range(PARTS):
            first.across(p, d)

    rows = spread(place_first, 256, False)
    for p in range(PARTS):
        first.complete(p)
        lo = 256 * p
        for group in range(8):
            here = slice(48 * group, 48 * group + 48)
            few = slice(16 * group, 16 * group + 16)
            laid = dot(rows, jnp.concatenate([held1[p, s] for s in members(p, group)], axis=0)).astype(BF16)
            for i in range(3):
                w_mod[here, 768 * i + lo : 768 * i + lo + 256] = laid[48 * i : 48 * i + 48]
            w_att[here, lo : lo + 256] = laid[144:192]
            if p == 0:
                w_att[here, 768:1024] = laid[192:240]
                bias[few, :] = laid[240:256, 0:128]
                cact_all[few, 0:128] = laid[240:256, 128:256]
            elif p == 1:
                w_att[here, 1024:1152] = laid[192:240, 0:128]
                w_out[here, 0:128] = laid[192:240, 128:256]
                cact_all[few, 128:384] = laid[240:256]
            else:
                w_out[here, 128:384] = laid[192:240]

    raw_bias = bias[...]
    modulation = jnp.concatenate(
        [total(w_mod[:, 128 * t : 128 * t + 128].astype(F32) * cact_column) for t in range(18)],
        axis=1,
    ) + bias_row(raw_bias, "mod", 6 * D)
    shift1, scale1, gate1, shift2, scale2, gate2 = [
        modulation[:, D * i : D * i + D] for i in range(6)
    ]
    hidden1 = (n1 * (1.0 + scale1) + shift1).astype(BF16)
    b_attend = bias_row(raw_bias, "attend", 2 * D)
    b_full = jnp.concatenate([b_attend[:, :D], jnp.zeros((1, D), F32), b_attend[:, D:]], axis=1)
    triple = (dot(hidden1, w_att[...]) + b_full).astype(BF16)

    def pair(i, which):
        lo = D * which + 128 * i
        return triple[:, lo : lo + 128]

    for d in (1, 3, 2):
        for p in range(PARTS):
            second.across(p, d)

    lane = lax.broadcasted_iota(jnp.int32, (S, 128), 1)
    halves = [lane < 64, lane >= 64]
    nothing = jnp.zeros((S, 128), BF16)
    mixed_pairs = []
    keys_t = []
    for i in range(3):
        q, k, v = pair(i, 0), pair(i, 1), pair(i, 2)
        v_t = v.T
        keys_t.append(k.T)
        mixed_t = []
        for h in range(2):
            scores = dot(k, jnp.where(halves[h], q, nothing), 1, 1) * FACTOR
            e = jnp.exp(scores - jnp.max(scores, axis=0, keepdims=True))
            probs = e * (1.0 / total(e))
            probs_ref[2 * i + h] = probs
            mixed_t.append(dot(v_t[64 * h : 64 * h + 64], probs.astype(BF16)))
        mixed_pairs.append(jnp.concatenate(mixed_t, axis=0).T.astype(BF16))
    mixed = jnp.concatenate(mixed_pairs, axis=1)
    branch = dot(mixed, w_out[...]) + bias_row(raw_bias, "output", D)
    middle = x + gate1 * branch
    n2, inverse2 = normalize(middle)
    hidden2 = (n2 * (1.0 + scale2) + shift2).astype(BF16)

    rows = spread(place_up, 96, False)
    left, right = spread(place_left, 192, False), spread(place_right, 192, False)
    for p in range(PARTS):
        second.complete(p)
    for group in range(8):
        here = slice(48 * group, 48 * group + 48)
        blocks = [jnp.concatenate([held2[p, s] for s in members(p, group)], axis=0) for p in range(PARTS)]
        for p in range(PARTS):
            laid = dot(rows, blocks[p]).astype(BF16)
            w_up[here, 256 * p : 256 * p + 256] = laid[0:48]
            w_up[here, 768 + 256 * p : 1024 + 256 * p] = laid[48:96]
        low = dot(left, jnp.concatenate([blocks[0], blocks[1][:, :128]], axis=1))
        high = dot(right, jnp.concatenate([blocks[1][:, 128:], blocks[2]], axis=1))
        w_down[192 * group : 192 * group + 192, :] = (low + high).astype(BF16)

    b_upper = bias_row(raw_bias, "up", FF)
    dfeed = (gate2 * g).astype(BF16)
    feed = jnp.zeros((S, D), F32)
    dhidden2 = jnp.zeros((S, D), F32)
    db_up = []
    hidden2_t = hidden2.T
    for c in range(4):
        lo = D * c
        upper = dot(hidden2, w_up[:, lo : lo + D]) + b_upper[:, lo : lo + D]
        square = upper * upper
        t = jnp.tanh(0.7978845608028654 * (upper + 0.044715 * (upper * square)))
        half = 0.5 * (1.0 + t)
        activated = (upper * half).astype(BF16)
        slope = half + (0.5 * upper) * (1.0 - t * t) * (
            0.7978845608028654 * (1.0 + 0.134145 * square)
        )
        feed = feed + dot(activated, w_down[lo : lo + D, :])
        dupper = (dot(dfeed, w_down[lo : lo + D, :], 1, 1) * slope).astype(BF16)
        d_down[lo : lo + D, :] = dot(activated.T, dfeed).astype(BF16)
        d_up[:, lo : lo + D] = dot(hidden2_t, dupper).astype(BF16)
        db_up.append(total(dupper.astype(F32)))
        dhidden2 = dhidden2 + dot(dupper, w_up[:, lo : lo + D], 1, 1)
    feed = feed + bias_row(raw_bias, "down", D)
    result[0] = (middle + gate2 * feed).astype(BF16)
    dgate2 = total(g * feed)
    db_down = total(dfeed.astype(F32))
    dscale2, dshift2 = total(dhidden2 * n2), total(dhidden2)
    gmid = g + denormalize(dhidden2 * (1.0 + scale2), n2, inverse2)
    dgate1 = total(gmid * branch)
    dbranch = (gate1 * gmid).astype(BF16)
    d_out[...] = dot(mixed.T, dbranch).astype(BF16)
    db_out = total(dbranch.astype(F32))

    rows = spread(place_back, 144, True)
    left, right = spread(place_left, 192, True), spread(place_right, 192, True)
    for p in range(PARTS):
        for group in range(8):
            here = slice(48 * group, 48 * group + 48)
            tall = slice(192 * group, 192 * group + 192)
            if p == 0:
                extra = d_out[here, 0:256]
                stretched = dot(left, d_down[tall, 0:256])
            elif p == 1:
                extra = jnp.concatenate([d_out[here, 256:384], jnp.zeros((48, 128), BF16)], axis=1)
                stretched = jnp.concatenate([dot(left, d_down[tall, 256:384]), dot(right, d_down[tall, 0:128])], axis=1)
            else:
                extra = jnp.zeros((48, 256), BF16)
                stretched = dot(right, d_down[tall, 128:384])
            flat = jnp.concatenate(
                [d_up[here, 256 * p : 256 * p + 256], d_up[here, 768 + 256 * p : 1024 + 256 * p], extra], axis=0
            )
            laid = (dot(rows, flat) + stretched).astype(BF16)
            for m, s in enumerate(members(p, group)):
                packed[p, s] = laid[16 * m : 16 * m + 16]
        back.across(p)

    dmixed = dot(dbranch, w_out[...], 1, 1).astype(BF16)

    dq, dk, dv = [], [], []
    for i in range(3):
        q, v = pair(i, 0), pair(i, 2)
        dm = dmixed[:, 128 * i : 128 * i + 128]
        dq_t, dk_h, dv_h = [], [], []
        for h in range(2):
            probs = probs_ref[2 * i + h]
            dprobs = dot(v, jnp.where(halves[h], dm, nothing), 1, 1)
            dv_h.append(dot(probs.astype(BF16), dm))
            dscores = (probs * (dprobs - total(probs * dprobs))).astype(BF16)
            dk_h.append(dot(dscores, q))
            dq_t.append(dot(keys_t[i][64 * h : 64 * h + 64], dscores))
        dq.append((jnp.concatenate(dq_t, axis=0).T * FACTOR).astype(BF16))
        dk.append((jnp.where(halves[0], dk_h[0], dk_h[1]) * FACTOR).astype(BF16))
        dv.append(jnp.where(halves[0], dv_h[0], dv_h[1]).astype(BF16))
        back.third(i)
    dtriple = jnp.concatenate(dq + dk + dv, axis=1)
    d_att[...] = dot(hidden1.T, dtriple).astype(BF16)
    sums = total(dtriple.astype(F32))
    db_att = jnp.concatenate([sums[:, :D], sums[:, 2 * D :]], axis=1)
    d_bias = (
        bias_block(db_att, "attend")
        + bias_block(db_out, "output")
        + bias_block(jnp.concatenate(db_up, axis=1), "up")
        + bias_block(db_down, "down")
    ).astype(BF16)
    rows = spread(place_attend, 160, True)
    for group in range(8):
        here = slice(48 * group, 48 * group + 48)
        biases = jnp.concatenate([d_bias[16 * group : 16 * group + 16], jnp.zeros((16, 256), BF16)], axis=1)
        flat = jnp.concatenate([d_att[here, 0:384], d_att[here, 384:768], d_att[here, 768:1152], biases], axis=0)
        laid = dot(rows, flat).astype(BF16)
        for p in range(PARTS):
            for m, s in enumerate(members(p, group)):
                packed_a[p, s] = laid[16 * m : 16 * m + 16, 128 * p : 128 * p + 128]
    for p in range(PARTS):
        last.across(p)

    dhidden1 = dot(dtriple, w_att[...], 1, 1)
    dscale1, dshift1 = total(dhidden1 * n1), total(dhidden1)
    dmods = [dshift1, dscale1, dgate1, dshift2, dscale2, dgate2]
    vectors = jnp.concatenate(dmods + [jnp.zeros((2, D), F32)], axis=0)
    for p in range(PARTS):
        held3[p, third.own(p)] = vectors[:, 128 * p : 128 * p + 128]
        third.first(p)
    for p in range(PARTS):
        last.third(p)
    for p in range(PARTS):
        back.second(p)
    token_grad[0] = gmid + denormalize(dhidden1 * (1.0 + scale1), n1, inverse1)
    for p in range(PARTS):
        third.second(p)

    dmod = jnp.concatenate(dmods, axis=1)
    dcact = jnp.zeros((D, 128), F32)
    for t in range(18):
        here = slice(128 * t, 128 * t + 128)
        dcact = dcact + w_mod[:, here].astype(F32) * dmod[:, here]
    condition_grad[...] = total(dcact.T) * (sigmoid * (1.0 + cond * (1.0 - sigmoid)))

    for p in range(PARTS):
        last.second(p)
    for p in range(PARTS):
        back.first(p)
    for p in range(PARTS):
        third.third(p)

    index = 2 * lax.axis_index("dp") + lax.axis_index("fsdp")
    feature = lax.broadcasted_iota(jnp.int32, (8, D), 1)
    r = lax.broadcasted_iota(jnp.int32, (8, D), 0)
    pick = jnp.where((feature == 3 * index + r) & (r < 3), 1.0, 0.0).astype(BF16)
    columns = dot(pick, cact_all[...], 1, 1).astype(BF16)
    natural = lax.broadcasted_iota(jnp.int32, (128, 1024), 0)
    j = lax.broadcasted_iota(jnp.int32, (128, 1024), 1) >> 3
    stacked = lax.broadcasted_iota(jnp.int32, (64, 1024), 0)
    inner = lax.broadcasted_iota(jnp.int32, (64, 1024), 1) & 7
    weighing = []
    for p in range(PARTS):
        a, b, c = ORDERS[p]
        coordinate = {c: (j >> 4) & 3, b: (j >> 2) & 3, a: j & 3}
        xj, yj, zj = coordinate[0], coordinate[1], coordinate[2]
        source = zj * 32 + (xj & 1) * 16 + yj * 4 + (j >> 6) * 2 + (xj >> 1)
        expanded = dot(columns, jnp.where(source == natural, 1.0, 0.0).astype(BF16))
        tiled = jnp.concatenate([expanded] * 8, axis=0)
        tiled = jnp.where((stacked & 7) == 3, 1.0, tiled)
        weighing.append(jnp.where((stacked >> 3) == inner, tiled, 0.0).astype(BF16))

    for p in range(PARTS):
        last.first(p)
    for p in range(PARTS):
        grad_ff[:, 256 * p : 256 * p + 256] = back.total(p)
    for d in (1, 3, 2):
        for p in range(PARTS):
            third.across(p, d)
    for p in range(PARTS):
        grad_att[:, 128 * p : 128 * p + 128] = last.total(p)
    weighed = []
    for p in range(PARTS):
        third.complete(p)
        weighed.append(dot(weighing[p], held3[p].reshape(1024, 128).astype(BF16)))
    grads = jnp.concatenate(
        [weighed[p][8 * i : 8 * i + 8] for i in range(6) for p in range(PARTS)], axis=1
    )
    n = lax.broadcasted_iota(jnp.int32, (6 * D, 128), 0)
    k = lax.broadcasted_iota(jnp.int32, (6 * D, 128), 1)
    mine = jnp.where((n == 18 * index + k) & (k < 18), 1.0, 0.0).astype(BF16)
    grad_mod[:, 0 : 6 * D] = grads
    grad_mod[:, 6 * D :] = dot(grads.astype(BF16), mine)
    for moves in (first, second, third, back, last):
        moves.sent()


def unpack_kernel(
    result_in, token_in, condition_in, ff, attend, modulation,
    result, token_grad, condition_grad, mod, b_mod, att, b_att, out, b_out, up, b_up, down, b_down,
):
    result[...] = result_in[...]
    token_grad[...] = token_in[...]
    condition_grad[...] = condition_in[...]
    mod[:, 0, :] = modulation[0:3, 0 : 6 * D]
    b_mod[...] = modulation[3:4, 6 * D : 6 * D + 18]
    for i in range(3):
        att[:, 0, D * i : D * i + D] = attend[3 * i : 3 * i + 3, :]
    for i in range(2):
        up[:, 0, 768 * i : 768 * i + 768] = ff[3 * i : 3 * i + 3, :]
        down[6 * i : 6 * i + 6, 0, :] = ff[6:12, D * i : D * i + D]
    out[:, 0, :] = ff[12:15, 0:D]
    for ref, name in ((b_att, "attend"), (b_out, "output"), (b_up, "up"), (b_down, "down")):
        size, _, lane = BIASES[name]
        ref[...] = attend[9:10, lane : lane + size]


def whole(count):
    return [pl.BlockSpec(memory_space=pltpu.VMEM)] * count


def shape(*dims, dtype=BF16):
    return jax.ShapeDtypeStruct(dims, dtype)


def reduce_scratch(wide):
    return [
        pltpu.VMEM((PARTS, 128, 16, wide), BF16),
        pltpu.VMEM((PARTS, 64, 16, wide), BF16),
        pltpu.VMEM((PARTS, 64, 16, wide), BF16),
        pltpu.VMEM((PARTS, 3, 16, 16, wide), BF16),
        pltpu.VMEM((PARTS, 16, 16, wide), BF16),
        pltpu.VMEM((PARTS, 3, 4, 16, wide), BF16),
        pltpu.VMEM((PARTS, 4, 16, wide), F32),
        pltpu.VMEM((PARTS, 4, 16, wide), BF16),
        pltpu.VMEM((PARTS, 3, 16, wide), BF16),
    ]


def local(*args):
    outs = [
        shape(1, S, D), shape(1, S, D, dtype=F32), shape(1, D, dtype=F32),
    ]
    computed = pl.pallas_call(
        block_kernel,
        out_shape=outs + [shape(16, 768, dtype=F32), shape(16, D, dtype=F32), shape(8, 6 * D + 128, dtype=F32)],
        in_specs=whole(13),
        out_specs=whole(6),
        scratch_shapes=[
            pltpu.VMEM((PARTS, 128, 16, 256), BF16),
            pltpu.VMEM((PARTS, 128, 16, 256), BF16),
            pltpu.VMEM((PARTS, 128, 8, 128), F32),
            pltpu.VMEM((D, 6 * D), BF16), pltpu.VMEM((D, 3 * D), BF16), pltpu.VMEM((D, D), BF16),
            pltpu.VMEM((D, FF), BF16), pltpu.VMEM((FF, D), BF16), pltpu.VMEM((128, 128), BF16), pltpu.VMEM((128, D), BF16),
            pltpu.VMEM((D, 3 * D), BF16), pltpu.VMEM((D, D), BF16),
            pltpu.VMEM((D, FF), BF16), pltpu.VMEM((FF, D), BF16), pltpu.VMEM((6, S, S), F32),
            *reduce_scratch(256),
            *reduce_scratch(128),
            pltpu.SemaphoreType.DMA((5, 2, 4, PARTS, 4)),
        ],
        compiler_params=pltpu.CompilerParams(
            collective_id=0, has_side_effects=True, vmem_limit_bytes=VMEM_LIMIT
        ),
    )(*args)
    grads = [
        shape(3, 1, 6 * D, dtype=F32), shape(1, 18, dtype=F32), shape(3, 1, 3 * D, dtype=F32),
        shape(1, 6, dtype=F32), shape(3, 1, D, dtype=F32), shape(1, 3, dtype=F32),
        shape(3, 1, FF, dtype=F32), shape(1, 12, dtype=F32), shape(12, 1, D, dtype=F32), shape(1, 3, dtype=F32),
    ]
    final = pl.pallas_call(
        unpack_kernel, out_shape=outs + grads, in_specs=whole(6), out_specs=whole(13)
    )(*computed)
    return tuple(
        jnp.swapaxes(item, 0, 1) if i >= 3 and item.ndim == 3 else item for i, item in enumerate(final)
    )


def solution(mesh):
    latents = P(("dp", "fsdp"), None, None)
    rows = P(None, ("dp", "fsdp"), None)
    entries = P(None, ("dp", "fsdp"))
    weights = (rows, entries) * 5
    return jax.shard_map(
        local,
        mesh=mesh,
        in_specs=(latents, P(("dp", "fsdp"), None), *weights, latents),
        out_specs=(latents, latents, P(("dp", "fsdp"), None), *weights),
        check_vma=False,
    )
```

```python
import jax
import jax.numpy as jnp
from jax import lax
from jax.experimental import pallas as pl
from jax.experimental.pallas import tpu as pltpu
from jax.sharding import PartitionSpec as P

MESH = pl.DeviceIdType.MESH
F32 = jnp.float32
BF16 = jnp.bfloat16
EPS = 1e-06
HEAD = 64
D = 384
FF = 1536
S = 256
FACTOR = HEAD ** (-0.5)
VMEM_LIMIT = 60 * 1024 * 1024

PARTS = 3
ORDERS = ((0, 1, 2), (1, 2, 0), (2, 0, 1))
BIASES = {"mod": (18, 0), "attend": (6, 18), "output": (3, 24), "up": (12, 27), "down": (3, 39)}


def dot(a, b, ca=1, cb=0):
    return lax.dot_general(a, b, (((ca,), (cb,)), ((), ())), preferred_element_type=F32)


def place():
    dp, fsdp = lax.axis_index("dp"), lax.axis_index("fsdp")
    core = lax.rem(dp, 2)
    y = lax.rem(lax.div(dp, 2), 4)
    x = lax.rem(lax.div(dp, 8), 2) + 2 * fsdp
    return (x, y, lax.div(dp, 16)), core


def device(at, core):
    x, y, z = at
    return (z * 16 + lax.rem(x, 2) * 8 + y * 2 + core, lax.div(x, 2))


def owner_of(at, core):
    x, y, z = at
    return z * 32 + (x & 1) * 16 + y * 4 + core * 2 + (x >> 1)


def moved(at, axis, by):
    return tuple(lax.rem(c + by, 4) if i == axis else c for i, c in enumerate(at))


def slot_of(part, x, y, z, core):
    at = (x, y, z)
    a, b, c = ORDERS[part]
    return ((core * 4 + at[c]) * 4 + at[b]) * 4 + at[a]


def announce(at, core):
    barrier = pltpu.get_barrier_semaphore()
    for axis in range(3):
        for by in range(1, 4):
            pl.semaphore_signal(
                barrier, inc=1, device_id=device(moved(at, axis, by), core), device_id_type=MESH
            )
    pl.semaphore_signal(barrier, inc=1, device_id=device(at, 1 - core), device_id_type=MESH)


class Moves:
    def __init__(self, at, core, send, recv):
        self.at, self.core, self.send, self.recv = at, core, send, recv
        self.copies = {}

    def start(self, stage, p, k, src, dst, axis, by):
        to = device(self.at, 1 - self.core) if axis is None else device(moved(self.at, axis, by), self.core)
        copy = pltpu.make_async_remote_copy(
            src_ref=src, dst_ref=dst, send_sem=self.send.at[stage, p, k], recv_sem=self.recv.at[stage, p, k],
            device_id=to, device_id_type=MESH,
        )
        copy.start()
        self.copies[stage, p, k] = copy

    def arrived(self, stage, p, ks):
        for k in ks:
            self.copies[stage, p, k].wait_recv()

    def sent(self):
        for copy in self.copies.values():
            copy.wait_send()


class Gather(Moves):
    def __init__(self, at, core, held, send, recv):
        super().__init__(at, core, send, recv)
        self.held = held

    def own(self, p):
        return slot_of(p, *self.at, self.core)

    def first(self, p):
        block = self.held.at[p, pl.ds(self.own(p), 1)]
        for d in (1, 3, 2):
            self.start(0, p, d, block, block, ORDERS[p][0], d)

    def second(self, p):
        self.arrived(0, p, (1, 3, 2))
        _, b, c = ORDERS[p]
        block = self.held.at[p, pl.ds(((self.core * 4 + self.at[c]) * 4 + self.at[b]) * 4, 4)]
        for d in (1, 3, 2):
            self.start(1, p, d, block, block, b, d)

    def plane(self, p, by):
        lo = (self.core * 4 + lax.rem(self.at[ORDERS[p][2]] + by, 4)) * 16
        return self.held.at[p, pl.ds(lo, 16)]

    def third(self, p):
        self.arrived(1, p, (1, 3, 2))
        block = self.plane(p, 0)
        for d in (1, 3, 2):
            self.start(2, p, d, block, block, ORDERS[p][2], d)
        self.start(3, p, 0, block, block, None, 0)

    def across(self, p, d):
        self.arrived(2, p, (d,))
        block = self.plane(p, 4 - d)
        self.start(3, p, d, block, block, None, 0)

    def complete(self, p):
        self.arrived(3, p, range(4))


def add(*blocks):
    out = blocks[0].astype(F32)
    for block in blocks[1:]:
        out = out + block.astype(F32)
    return out


class Reduce(Moves):
    def __init__(self, at, core, packed, chip, ours, ring, joined, row, near, line, ends, send, recv):
        super().__init__(at, core, send, recv)
        self.packed, self.chip, self.ours, self.ring, self.joined = packed, chip, ours, ring, joined
        self.row, self.near, self.line, self.ends = row, near, line, ends

    def chunk(self, p, by):
        return lax.rem(self.at[ORDERS[p][2]] + by, 4) * 16

    def across(self, p):
        self.start(0, p, 0, self.packed.at[p, pl.ds((1 - self.core) * 64, 64)], self.chip.at[p], None, 0)

    def third(self, p):
        self.arrived(0, p, (0,))
        for by in (2, 1, 3, 0):
            lo = self.chunk(p, by)
            here = pl.ds(lo, 16)
            self.ours[p, here] = self.packed[p, pl.ds(self.core * 64 + lo, 16)] + self.chip[p, here]
            if by:
                self.start(1, p, by, self.ours.at[p, here], self.ring.at[p, by - 1], ORDERS[p][2], by)

    def second(self, p, more=None):
        self.arrived(1, p, (1, 3, 2))
        ring = self.ring
        wide = ring.shape[-1]
        summed = add(self.ours[p, pl.ds(self.chunk(p, 0), 16)], ring[p, 0], ring[p, 1], ring[p, 2]).astype(BF16)
        self.joined[p, :, :, 0:wide] = summed
        if more is not None:
            self.joined[p, :, :, wide:] = more
        b = ORDERS[p][1]
        for d in (2, 1, 3):
            src = self.joined.at[p, pl.ds(lax.rem(self.at[b] + d, 4) * 4, 4)]
            self.start(2, p, d, src, self.row.at[p, d - 1], b, d)

    def first(self, p):
        self.arrived(2, p, (1, 3, 2))
        a, b, _ = ORDERS[p]
        row = self.row
        self.near[p] = add(self.joined[p, pl.ds(self.at[b] * 4, 4)], row[p, 0], row[p, 1], row[p, 2])
        self.line[p] = self.near[p].astype(BF16)
        for d in (2, 1, 3):
            src = self.line.at[p, pl.ds(lax.rem(self.at[a] + d, 4), 1)]
            self.start(3, p, d, src, self.ends.at[p, pl.ds(d - 1, 1)], a, d)

    def total(self, p):
        self.arrived(3, p, (1, 3, 2))
        ends = self.ends
        return add(self.near[p, self.at[ORDERS[p][0]]], ends[p, 0], ends[p, 1], ends[p, 2])


def spread(place_of, count, transposed):
    shape = (256, count) if transposed else (count, 256)
    n = lax.broadcasted_iota(jnp.int32, shape, 0 if transposed else 1)
    o = lax.broadcasted_iota(jnp.int32, shape, 1 if transposed else 0)
    return jnp.where(place_of(n >> 4, n & 15) == o, 1.0, 0.0).astype(BF16)


def threes(member, row):
    section = (row * 11) >> 5
    return section * 48 + member * 3 + (row - 3 * section)


def place_first(member, row):
    return jnp.where(row == 15, 240 + member, threes(member, row))


def place_up(member, row):
    return jnp.where(row < 6, threes(member, row), -1)


def place_left(member, row):
    return jnp.where((row >= 6) & (row < 12), member * 12 + row - 6, -1)


def place_right(member, row):
    return jnp.where((row >= 6) & (row < 12), member * 12 + row, -1)


def place_back(member, row):
    return jnp.where(row < 6, threes(member, row), jnp.where((row >= 12) & (row < 15), threes(member, row) - 96, -1))


def place_attend(member, row):
    return jnp.where(row < 9, threes(member, row), jnp.where(row == 9, 144 + member, -1))


def members(part, group):
    z, x_lo = group // 2, group % 2
    return [
        slot_of(part, 2 * x_hi + x_lo, y, z, core)
        for y in range(4)
        for core in range(2)
        for x_hi in range(2)
    ]


def bias_map(name, count, lane):
    size = BIASES[name][0]
    n = lax.broadcasted_iota(jnp.int32, (128, count), 1)
    owner = (n * -(-65536 // size)) >> 16
    k = lax.broadcasted_iota(jnp.int32, (128, count), 0)
    return owner == k, (n - owner * size + lane) == k


def bias_row(bias, name, count):
    mine, lane = bias_map(name, count, BIASES[name][1])
    picked = dot(bias, jnp.where(lane, 1.0, 0.0).astype(BF16))
    return jnp.sum(jnp.where(mine, picked, 0.0), axis=0, keepdims=True)


def bias_block(row, name):
    mine, lane = bias_map(name, row.shape[1], BIASES[name][1])
    placed = jnp.where(mine, row, 0.0).astype(BF16)
    return dot(placed, jnp.where(lane, 1.0, 0.0).astype(BF16), 1, 1)


def weighing(p, at, core, cact_all):
    a, b, c = ORDERS[p]

    def along(c_at, core_at, b_at, a_at):
        spot = {c: c_at, b: b_at, a: a_at}
        return owner_of((spot[0], spot[1], spot[2]), core_at)

    latent = lax.broadcasted_iota(jnp.int32, (64, 128), 0) >> 3
    here = along(latent >> 1, latent & 1, at[b], at[a])
    pick = jnp.where(here == lax.broadcasted_iota(jnp.int32, (64, 128), 1), 1.0, 0.0).astype(BF16)
    cacts = dot(pick, cact_all).astype(BF16)
    n = lax.broadcasted_iota(jnp.int32, (256, D), 0)
    row = n & 15
    section = (row * 11) >> 5
    feature = 3 * along(at[c], core, n >> 6, (n >> 4) & 3) + row - 3 * section
    chosen = jnp.where((feature == lax.broadcasted_iota(jnp.int32, (256, D), 1)) & (row < 9), 1.0, 0.0).astype(BF16)
    weights = dot(chosen, cacts, 1, 1)
    row = lax.broadcasted_iota(jnp.int32, (256, 64), 0) & 15
    return jnp.where((row * 11) >> 5 == (lax.broadcasted_iota(jnp.int32, (256, 64), 1) & 7), weights, 0.0).astype(BF16)


def normalize(v):
    shifted = v - jnp.mean(v, axis=-1, keepdims=True)
    inverse = lax.rsqrt(jnp.mean(shifted * shifted, axis=-1, keepdims=True) + EPS)
    return shifted * inverse, inverse


def denormalize(e, n, inverse):
    return inverse * (
        e - jnp.mean(e, axis=-1, keepdims=True) - n * jnp.mean(e * n, axis=-1, keepdims=True)
    )


def total(v):
    return jnp.sum(v, axis=0, keepdims=True)


def block_kernel(
    tokens, condition, mod, b_mod, att, b_att, out, b_out, up, b_up, down, b_down, cotangent,
    result, token_grad, condition_grad, grad_ff, grad_att, grad_mod,
    held1, held2, pair_vectors, vectors, w_mod, w_att, w_out, w_up, w_down, bias, cact_all,
    d_att, d_out, d_up, d_down, probs_ref,
    packed, chip, ours, ring, joined, row, near, line, ends,
    packed_a, chip_a, ours_a, ring_a, joined_a, row_a, near_a, line_a, ends_a,
    sems,
):
    at, core = place()
    announce(at, core)
    first, second = [Gather(at, core, held, sems.at[i, 0], sems.at[i, 1]) for i, held in enumerate((held1, held2))]
    trade = Moves(at, core, sems.at[2, 0], sems.at[2, 1])
    back = Reduce(at, core, packed, chip, ours, ring, joined, row, near, line, ends, sems.at[3, 0], sems.at[3, 1])
    last = Reduce(
        at, core, packed_a, chip_a, ours_a, ring_a, joined_a, row_a, near_a, line_a, ends_a, sems.at[4, 0], sems.at[4, 1]
    )

    def load(ref, lo, hi):
        return ref[0, :, lo:hi].astype(F32)

    cond = condition[...].astype(F32)
    sigmoid = 1.0 / (1.0 + jnp.exp(-cond))
    cact = (cond * sigmoid).astype(BF16).astype(F32)
    bias_line = jnp.concatenate(
        [ref[...].astype(F32) for ref in (b_mod, b_att, b_out, b_up, b_down)]
        + [jnp.zeros((1, 128 - 42), F32), cact, jnp.zeros((1, 256), F32)],
        axis=1,
    )
    mine = jnp.concatenate(
        [load(mod, 0, 768), load(mod, 768, 1536), load(mod, 1536, 2304), load(att, 0, 768),
         jnp.concatenate([load(att, 768, 1152), load(out, 0, 384)], axis=1), bias_line],
        axis=0,
    ).astype(BF16)
    tall = down[0].astype(F32)
    mine2 = jnp.concatenate(
        [load(up, 0, 768), load(up, 768, 1536), jnp.concatenate([tall[0:6], tall[6:12]], axis=1), jnp.zeros((4, 768), F32)],
        axis=0,
    ).astype(BF16)
    for p in range(PARTS):
        held1[p, first.own(p)] = mine[:, 256 * p : 256 * p + 256]
        held2[p, second.own(p)] = mine2[:, 256 * p : 256 * p + 256]

    pl.semaphore_wait(pltpu.get_barrier_semaphore(), 10)
    for p in range(PARTS):
        first.first(p)
    for p in range(PARTS):
        second.first(p)

    x = tokens[0].astype(F32)
    g = cotangent[0].astype(F32)
    cact_column = jnp.broadcast_to(cact, (128, D)).T
    n1, inverse1 = normalize(x)

    for p in range(PARTS):
        first.second(p)
    for p in range(PARTS):
        second.second(p)
    for p in range(PARTS):
        first.third(p)
    for p in range(PARTS):
        second.third(p)
    for d in (1, 3, 2):
        for p in range(PARTS):
            first.across(p, d)

    rows = spread(place_first, 256, False)
    for p in range(PARTS):
        first.complete(p)
        lo = 256 * p
        for group in range(8):
            here = slice(48 * group, 48 * group + 48)
            few = slice(16 * group, 16 * group + 16)
            laid = dot(rows, jnp.concatenate([held1[p, s] for s in members(p, group)], axis=0)).astype(BF16)
            for i in range(3):
                w_mod[here, 768 * i + lo : 768 * i + lo + 256] = laid[48 * i : 48 * i + 48]
            w_att[here, lo : lo + 256] = laid[144:192]
            if p == 0:
                w_att[here, 768:1024] = laid[192:240]
                bias[few, :] = laid[240:256, 0:128]
                cact_all[few, 0:128] = laid[240:256, 128:256]
            elif p == 1:
                w_att[here, 1024:1152] = laid[192:240, 0:128]
                w_out[here, 0:128] = laid[192:240, 128:256]
                cact_all[few, 128:384] = laid[240:256]
            else:
                w_out[here, 128:384] = laid[192:240]

    raw_bias = bias[...]
    modulation = jnp.concatenate(
        [total(w_mod[:, 128 * t : 128 * t + 128].astype(F32) * cact_column) for t in range(18)],
        axis=1,
    ) + bias_row(raw_bias, "mod", 6 * D)
    shift1, scale1, gate1, shift2, scale2, gate2 = [
        modulation[:, D * i : D * i + D] for i in range(6)
    ]
    hidden1 = (n1 * (1.0 + scale1) + shift1).astype(BF16)
    b_attend = bias_row(raw_bias, "attend", 2 * D)
    b_full = jnp.concatenate([b_attend[:, :D], jnp.zeros((1, D), F32), b_attend[:, D:]], axis=1)
    triple = (dot(hidden1, w_att[...]) + b_full).astype(BF16)

    def pair(i, which):
        lo = D * which + 128 * i
        return triple[:, lo : lo + 128]

    for d in (1, 3, 2):
        for p in range(PARTS):
            second.across(p, d)

    lane = lax.broadcasted_iota(jnp.int32, (S, 128), 1)
    halves = [lane < 64, lane >= 64]
    nothing = jnp.zeros((S, 128), BF16)
    mixed_pairs = []
    keys_t = []
    for i in range(3):
        q, k, v = pair(i, 0), pair(i, 1), pair(i, 2)
        v_t = v.T
        keys_t.append(k.T)
        mixed_t = []
        for h in range(2):
            scores = dot(k, jnp.where(halves[h], q, nothing), 1, 1) * FACTOR
            e = jnp.exp(scores - jnp.max(scores, axis=0, keepdims=True))
            probs = e * (1.0 / total(e))
            probs_ref[2 * i + h] = probs
            mixed_t.append(dot(v_t[64 * h : 64 * h + 64], probs.astype(BF16)))
        mixed_pairs.append(jnp.concatenate(mixed_t, axis=0).T.astype(BF16))
    mixed = jnp.concatenate(mixed_pairs, axis=1)
    branch = dot(mixed, w_out[...]) + bias_row(raw_bias, "output", D)
    middle = x + gate1 * branch
    n2, inverse2 = normalize(middle)
    hidden2 = (n2 * (1.0 + scale2) + shift2).astype(BF16)

    rows = spread(place_up, 96, False)
    left, right = spread(place_left, 192, False), spread(place_right, 192, False)
    for p in range(PARTS):
        second.complete(p)
    for group in range(8):
        here = slice(48 * group, 48 * group + 48)
        blocks = [jnp.concatenate([held2[p, s] for s in members(p, group)], axis=0) for p in range(PARTS)]
        for p in range(PARTS):
            laid = dot(rows, blocks[p]).astype(BF16)
            w_up[here, 256 * p : 256 * p + 256] = laid[0:48]
            w_up[here, 768 + 256 * p : 1024 + 256 * p] = laid[48:96]
        low = dot(left, jnp.concatenate([blocks[0], blocks[1][:, :128]], axis=1))
        high = dot(right, jnp.concatenate([blocks[1][:, 128:], blocks[2]], axis=1))
        w_down[192 * group : 192 * group + 192, :] = (low + high).astype(BF16)

    weights = [weighing(p, at, core, cact_all[...]) for p in range(PARTS)]
    b_upper = bias_row(raw_bias, "up", FF)
    dfeed = (gate2 * g).astype(BF16)
    feed = jnp.zeros((S, D), F32)
    dhidden2 = jnp.zeros((S, D), F32)
    db_up = []
    hidden2_t = hidden2.T
    for c in range(4):
        lo = D * c
        upper = dot(hidden2, w_up[:, lo : lo + D]) + b_upper[:, lo : lo + D]
        square = upper * upper
        t = jnp.tanh(0.7978845608028654 * (upper + 0.044715 * (upper * square)))
        half = 0.5 * (1.0 + t)
        activated = (upper * half).astype(BF16)
        slope = half + (0.5 * upper) * (1.0 - t * t) * (
            0.7978845608028654 * (1.0 + 0.134145 * square)
        )
        feed = feed + dot(activated, w_down[lo : lo + D, :])
        dupper = (dot(dfeed, w_down[lo : lo + D, :], 1, 1) * slope).astype(BF16)
        d_down[lo : lo + D, :] = dot(activated.T, dfeed).astype(BF16)
        d_up[:, lo : lo + D] = dot(hidden2_t, dupper).astype(BF16)
        db_up.append(total(dupper.astype(F32)))
        dhidden2 = dhidden2 + dot(dupper, w_up[:, lo : lo + D], 1, 1)
    feed = feed + bias_row(raw_bias, "down", D)
    result[0] = (middle + gate2 * feed).astype(BF16)
    dgate2 = total(g * feed)
    db_down = total(dfeed.astype(F32))
    dscale2, dshift2 = total(dhidden2 * n2), total(dhidden2)
    gmid = g + denormalize(dhidden2 * (1.0 + scale2), n2, inverse2)
    dgate1 = total(gmid * branch)
    dbranch = (gate1 * gmid).astype(BF16)
    d_out[...] = dot(mixed.T, dbranch).astype(BF16)
    db_out = total(dbranch.astype(F32))

    rows = spread(place_back, 144, True)
    left, right = spread(place_left, 192, True), spread(place_right, 192, True)
    for p in range(PARTS):
        for group in range(8):
            here = slice(48 * group, 48 * group + 48)
            tall = slice(192 * group, 192 * group + 192)
            if p == 0:
                extra = d_out[here, 0:256]
                stretched = dot(left, d_down[tall, 0:256])
            elif p == 1:
                extra = jnp.concatenate([d_out[here, 256:384], jnp.zeros((48, 128), BF16)], axis=1)
                stretched = jnp.concatenate([dot(left, d_down[tall, 256:384]), dot(right, d_down[tall, 0:128])], axis=1)
            else:
                extra = jnp.zeros((48, 256), BF16)
                stretched = dot(right, d_down[tall, 128:384])
            flat = jnp.concatenate(
                [d_up[here, 256 * p : 256 * p + 256], d_up[here, 768 + 256 * p : 1024 + 256 * p], extra], axis=0
            )
            laid = (dot(rows, flat) + stretched).astype(BF16)
            for m, s in enumerate(members(p, group)):
                packed[p, s] = laid[16 * m : 16 * m + 16]
        back.across(p)

    dmixed = dot(dbranch, w_out[...], 1, 1).astype(BF16)

    dq, dk, dv = [], [], []
    for i in range(3):
        q, v = pair(i, 0), pair(i, 2)
        dm = dmixed[:, 128 * i : 128 * i + 128]
        dq_t, dk_h, dv_h = [], [], []
        for h in range(2):
            probs = probs_ref[2 * i + h]
            dprobs = dot(v, jnp.where(halves[h], dm, nothing), 1, 1)
            dv_h.append(dot(probs.astype(BF16), dm))
            dscores = (probs * (dprobs - total(probs * dprobs))).astype(BF16)
            dk_h.append(dot(dscores, q))
            dq_t.append(dot(keys_t[i][64 * h : 64 * h + 64], dscores))
        dq.append((jnp.concatenate(dq_t, axis=0).T * FACTOR).astype(BF16))
        dk.append((jnp.where(halves[0], dk_h[0], dk_h[1]) * FACTOR).astype(BF16))
        dv.append(jnp.where(halves[0], dv_h[0], dv_h[1]).astype(BF16))
        if i == 1:
            back.third(0)
            back.third(1)
    back.third(2)
    dtriple = jnp.concatenate(dq + dk + dv, axis=1)
    dhidden1 = dot(dtriple, w_att[...], 1, 1)
    dscale1, dshift1 = total(dhidden1 * n1), total(dhidden1)
    dmod = jnp.concatenate([dshift1, dscale1, dgate1, dshift2, dscale2, dgate2], axis=1)
    sections = jnp.concatenate([dmod[:, 768 * i : 768 * i + 768] for i in range(3)] + [jnp.zeros((5, 768), F32)], axis=0)
    for p in range(PARTS):
        pair_vectors[core, p] = sections[:, 256 * p : 256 * p + 256]
    trade.start(0, 0, 0, pair_vectors.at[core], pair_vectors.at[core], None, 0)
    d_att[...] = dot(hidden1.T, dtriple).astype(BF16)
    sums = total(dtriple.astype(F32))
    db_att = jnp.concatenate([sums[:, :D], sums[:, 2 * D :]], axis=1)
    d_bias = (
        bias_block(dmod, "mod")
        + bias_block(db_att, "attend")
        + bias_block(db_out, "output")
        + bias_block(jnp.concatenate(db_up, axis=1), "up")
        + bias_block(db_down, "down")
    ).astype(BF16)
    rows = spread(place_attend, 160, True)
    for group in range(8):
        here = slice(48 * group, 48 * group + 48)
        biases = jnp.concatenate([d_bias[16 * group : 16 * group + 16], jnp.zeros((16, 256), BF16)], axis=1)
        flat = jnp.concatenate([d_att[here, 0:384], d_att[here, 384:768], d_att[here, 768:1152], biases], axis=0)
        laid = dot(rows, flat).astype(BF16)
        for p in range(PARTS):
            for m, s in enumerate(members(p, group)):
                packed_a[p, s] = laid[16 * m : 16 * m + 16, 128 * p : 128 * p + 128]
    for p in range(PARTS):
        last.across(p)

    trade.arrived(0, 0, (0,))
    for p in range(PARTS):
        c = ORDERS[p][2]
        for d in (1, 3, 2):
            trade.start(1, p, d, pair_vectors.at[:, p], vectors.at[p, at[c]], c, d)
        vectors[p, at[c]] = pair_vectors[:, p]
    for p in range(PARTS):
        last.third(p)
    for p in range(PARTS):
        back.second(p)
    token_grad[0] = gmid + denormalize(dhidden1 * (1.0 + scale1), n1, inverse1)
    dcact = jnp.zeros((D, 128), F32)
    for t in range(18):
        here = slice(128 * t, 128 * t + 128)
        dcact = dcact + w_mod[:, here].astype(F32) * dmod[:, here]
    condition_grad[...] = total(dcact.T) * (sigmoid * (1.0 + cond * (1.0 - sigmoid)))

    for p in range(PARTS):
        trade.arrived(1, p, (1, 3, 2))
    d_mod = [dot(weights[p], vectors[p].reshape(64, 256).astype(BF16)).astype(BF16) for p in range(PARTS)]
    for p in range(PARTS):
        last.second(p, d_mod[p].reshape(16, 16, 256))
    for p in range(PARTS):
        back.first(p)
    for p in range(PARTS):
        last.first(p)
    for p in range(PARTS):
        grad_ff[:, 256 * p : 256 * p + 256] = back.total(p)
    for p in range(PARTS):
        summed = last.total(p)
        grad_att[:, 128 * p : 128 * p + 128] = summed[:, 0:128]
        grad_mod[:, 256 * p : 256 * p + 256] = summed[:, 128:384]
    for moves in (first, second, trade, back, last):
        moves.sent()


def unpack_kernel(
    result_in, token_in, condition_in, ff, attend, modulation,
    result, token_grad, condition_grad, mod, b_mod, att, b_att, out, b_out, up, b_up, down, b_down,
):
    result[...] = result_in[...]
    token_grad[...] = token_in[...]
    condition_grad[...] = condition_in[...]
    for i in range(3):
        mod[:, 0, 768 * i : 768 * i + 768] = modulation[3 * i : 3 * i + 3, :]
        att[:, 0, D * i : D * i + D] = attend[3 * i : 3 * i + 3, :]
    for i in range(2):
        up[:, 0, 768 * i : 768 * i + 768] = ff[3 * i : 3 * i + 3, :]
        down[6 * i : 6 * i + 6, 0, :] = ff[6:12, D * i : D * i + D]
    out[:, 0, :] = ff[12:15, 0:D]
    for ref, name in ((b_mod, "mod"), (b_att, "attend"), (b_out, "output"), (b_up, "up"), (b_down, "down")):
        size, lane = BIASES[name]
        ref[...] = attend[9:10, lane : lane + size]


def whole(count):
    return [pl.BlockSpec(memory_space=pltpu.VMEM)] * count


def shape(*dims, dtype=BF16):
    return jax.ShapeDtypeStruct(dims, dtype)


def reduce_scratch(wide, wider):
    return [
        pltpu.VMEM((PARTS, 128, 16, wide), BF16),
        pltpu.VMEM((PARTS, 64, 16, wide), BF16),
        pltpu.VMEM((PARTS, 64, 16, wide), BF16),
        pltpu.VMEM((PARTS, 3, 16, 16, wide), BF16),
        pltpu.VMEM((PARTS, 16, 16, wider), BF16),
        pltpu.VMEM((PARTS, 3, 4, 16, wider), BF16),
        pltpu.VMEM((PARTS, 4, 16, wider), F32),
        pltpu.VMEM((PARTS, 4, 16, wider), BF16),
        pltpu.VMEM((PARTS, 3, 16, wider), BF16),
    ]


def local(*args):
    outs = [
        shape(1, S, D), shape(1, S, D, dtype=F32), shape(1, D, dtype=F32),
    ]
    computed = pl.pallas_call(
        block_kernel,
        out_shape=outs + [shape(16, 768, dtype=F32), shape(16, D, dtype=F32), shape(16, 768, dtype=F32)],
        in_specs=whole(13),
        out_specs=whole(6),
        scratch_shapes=[
            pltpu.VMEM((PARTS, 128, 16, 256), BF16),
            pltpu.VMEM((PARTS, 128, 16, 256), BF16),
            pltpu.VMEM((2, PARTS, 8, 256), F32),
            pltpu.VMEM((PARTS, 4, 2, 8, 256), F32),
            pltpu.VMEM((D, 6 * D), BF16), pltpu.VMEM((D, 3 * D), BF16), pltpu.VMEM((D, D), BF16),
            pltpu.VMEM((D, FF), BF16), pltpu.VMEM((FF, D), BF16), pltpu.VMEM((128, 128), BF16), pltpu.VMEM((128, D), BF16),
            pltpu.VMEM((D, 3 * D), BF16), pltpu.VMEM((D, D), BF16),
            pltpu.VMEM((D, FF), BF16), pltpu.VMEM((FF, D), BF16), pltpu.VMEM((6, S, S), F32),
            *reduce_scratch(256, 256),
            *reduce_scratch(128, 384),
            pltpu.SemaphoreType.DMA((5, 2, 4, PARTS, 4)),
        ],
        compiler_params=pltpu.CompilerParams(
            collective_id=0, has_side_effects=True, vmem_limit_bytes=VMEM_LIMIT
        ),
    )(*args)
    grads = [
        shape(3, 1, 6 * D, dtype=F32), shape(1, 18, dtype=F32), shape(3, 1, 3 * D, dtype=F32),
        shape(1, 6, dtype=F32), shape(3, 1, D, dtype=F32), shape(1, 3, dtype=F32),
        shape(3, 1, FF, dtype=F32), shape(1, 12, dtype=F32), shape(12, 1, D, dtype=F32), shape(1, 3, dtype=F32),
    ]
    final = pl.pallas_call(
        unpack_kernel, out_shape=outs + grads, in_specs=whole(6), out_specs=whole(13)
    )(*computed)
    return tuple(
        jnp.swapaxes(item, 0, 1) if i >= 3 and item.ndim == 3 else item for i, item in enumerate(final)
    )


def solution(mesh):
    latents = P(("dp", "fsdp"), None, None)
    rows = P(None, ("dp", "fsdp"), None)
    entries = P(None, ("dp", "fsdp"))
    weights = (rows, entries) * 5
    return jax.shard_map(
        local,
        mesh=mesh,
        in_specs=(latents, P(("dp", "fsdp"), None), *weights, latents),
        out_specs=(latents, latents, P(("dp", "fsdp"), None), *weights),
        check_vma=False,
    )
```

```python
import jax
import jax.numpy as jnp
from jax import lax
from jax.experimental import pallas as pl
from jax.experimental.pallas import tpu as pltpu
from jax.sharding import PartitionSpec as P

MESH = pl.DeviceIdType.MESH
F32 = jnp.float32
BF16 = jnp.bfloat16
EPS = 1e-06
HEAD = 64
D = 384
FF = 1536
S = 256
FACTOR = HEAD ** (-0.5)
VMEM_LIMIT = 60 * 1024 * 1024

PARTS = 3
ORDERS = ((0, 1, 2), (1, 2, 0), (2, 0, 1))
BIASES = {"mod": (18, 0), "attend": (6, 18), "output": (3, 24), "up": (12, 27), "down": (3, 39)}


def dot(a, b, ca=1, cb=0):
    return lax.dot_general(a, b, (((ca,), (cb,)), ((), ())), preferred_element_type=F32)


def place():
    dp, fsdp = lax.axis_index("dp"), lax.axis_index("fsdp")
    core = lax.rem(dp, 2)
    y = lax.rem(lax.div(dp, 2), 4)
    x = lax.rem(lax.div(dp, 8), 2) + 2 * fsdp
    return (x, y, lax.div(dp, 16)), core


def device(at, core):
    x, y, z = at
    return (z * 16 + lax.rem(x, 2) * 8 + y * 2 + core, lax.div(x, 2))


def owner_of(at, core):
    x, y, z = at
    return z * 32 + (x & 1) * 16 + y * 4 + core * 2 + (x >> 1)


def moved(at, axis, by):
    return tuple(lax.rem(c + by, 4) if i == axis else c for i, c in enumerate(at))


def slot_of(part, x, y, z, core):
    at = (x, y, z)
    a, b, c = ORDERS[part]
    return ((core * 4 + at[c]) * 4 + at[b]) * 4 + at[a]


def announce(at, core):
    barrier = pltpu.get_barrier_semaphore()
    for axis in range(3):
        for by in range(1, 4):
            pl.semaphore_signal(
                barrier, inc=1, device_id=device(moved(at, axis, by), core), device_id_type=MESH
            )
    pl.semaphore_signal(barrier, inc=1, device_id=device(at, 1 - core), device_id_type=MESH)


class Moves:
    def __init__(self, at, core, send, recv):
        self.at, self.core, self.send, self.recv = at, core, send, recv
        self.copies = {}

    def start(self, stage, p, k, src, dst, axis, by):
        to = device(self.at, 1 - self.core) if axis is None else device(moved(self.at, axis, by), self.core)
        copy = pltpu.make_async_remote_copy(
            src_ref=src, dst_ref=dst, send_sem=self.send.at[stage, p, k], recv_sem=self.recv.at[stage, p, k],
            device_id=to, device_id_type=MESH,
        )
        copy.start()
        self.copies[stage, p, k] = copy

    def arrived(self, stage, p, ks):
        for k in ks:
            self.copies[stage, p, k].wait_recv()

    def sent(self):
        for copy in self.copies.values():
            copy.wait_send()


class Gather(Moves):
    def __init__(self, at, core, held, send, recv):
        super().__init__(at, core, send, recv)
        self.held = held

    def own(self, p):
        return slot_of(p, *self.at, self.core)

    def first(self, p):
        block = self.held.at[p, pl.ds(self.own(p), 1)]
        for d in (1, 3, 2):
            self.start(0, p, d, block, block, ORDERS[p][0], d)

    def second(self, p):
        self.arrived(0, p, (1, 3, 2))
        _, b, c = ORDERS[p]
        block = self.held.at[p, pl.ds(((self.core * 4 + self.at[c]) * 4 + self.at[b]) * 4, 4)]
        for d in (1, 3, 2):
            self.start(1, p, d, block, block, b, d)

    def plane(self, p, by):
        lo = (self.core * 4 + lax.rem(self.at[ORDERS[p][2]] + by, 4)) * 16
        return self.held.at[p, pl.ds(lo, 16)]

    def third(self, p):
        self.arrived(1, p, (1, 3, 2))
        block = self.plane(p, 0)
        for d in (1, 3, 2):
            self.start(2, p, d, block, block, ORDERS[p][2], d)
        self.start(3, p, 0, block, block, None, 0)

    def across(self, p, d):
        self.arrived(2, p, (d,))
        block = self.plane(p, 4 - d)
        self.start(3, p, d, block, block, None, 0)

    def complete(self, p):
        self.arrived(3, p, range(4))


def add(*blocks):
    out = blocks[0].astype(F32)
    for block in blocks[1:]:
        out = out + block.astype(F32)
    return out


class Reduce(Moves):
    def __init__(self, at, core, packed, chip, ours, ring, joined, row, near, line, ends, send, recv):
        super().__init__(at, core, send, recv)
        self.packed, self.chip, self.ours, self.ring, self.joined = packed, chip, ours, ring, joined
        self.row, self.near, self.line, self.ends = row, near, line, ends

    def chunk(self, p, by):
        return lax.rem(self.at[ORDERS[p][2]] + by, 4) * 16

    def across(self, p):
        self.start(0, p, 0, self.packed.at[p, pl.ds((1 - self.core) * 64, 64)], self.chip.at[p], None, 0)

    def third(self, p):
        self.arrived(0, p, (0,))
        for by in (2, 1, 3, 0):
            lo = self.chunk(p, by)
            here = pl.ds(lo, 16)
            self.ours[p, here] = self.packed[p, pl.ds(self.core * 64 + lo, 16)] + self.chip[p, here]
            if by:
                self.start(1, p, by, self.ours.at[p, here], self.ring.at[p, by - 1], ORDERS[p][2], by)

    def second(self, p, more=None):
        self.arrived(1, p, (1, 3, 2))
        ring = self.ring
        wide = ring.shape[-1]
        summed = add(self.ours[p, pl.ds(self.chunk(p, 0), 16)], ring[p, 0], ring[p, 1], ring[p, 2]).astype(BF16)
        self.joined[p, :, :, 0:wide] = summed
        if more is not None:
            self.joined[p, :, :, wide:] = more
        b = ORDERS[p][1]
        for d in (2, 1, 3):
            src = self.joined.at[p, pl.ds(lax.rem(self.at[b] + d, 4) * 4, 4)]
            self.start(2, p, d, src, self.row.at[p, d - 1], b, d)

    def first(self, p):
        self.arrived(2, p, (1, 3, 2))
        a, b, _ = ORDERS[p]
        row = self.row
        self.near[p] = add(self.joined[p, pl.ds(self.at[b] * 4, 4)], row[p, 0], row[p, 1], row[p, 2])
        self.line[p] = self.near[p].astype(BF16)
        for d in (2, 1, 3):
            src = self.line.at[p, pl.ds(lax.rem(self.at[a] + d, 4), 1)]
            self.start(3, p, d, src, self.ends.at[p, pl.ds(d - 1, 1)], a, d)

    def total(self, p):
        self.arrived(3, p, (1, 3, 2))
        ends = self.ends
        return add(self.near[p, self.at[ORDERS[p][0]]], ends[p, 0], ends[p, 1], ends[p, 2])


def spread(place_of, count, transposed):
    shape = (256, count) if transposed else (count, 256)
    n = lax.broadcasted_iota(jnp.int32, shape, 0 if transposed else 1)
    o = lax.broadcasted_iota(jnp.int32, shape, 1 if transposed else 0)
    return jnp.where(place_of(n >> 4, n & 15) == o, 1.0, 0.0).astype(BF16)


def threes(member, row):
    section = (row * 11) >> 5
    return section * 48 + member * 3 + (row - 3 * section)


def place_first(member, row):
    return jnp.where(row == 15, 240 + member, threes(member, row))


def shuffle(transposed):
    n = lax.broadcasted_iota(jnp.int32, (D, D), 0 if transposed else 1)
    o = lax.broadcasted_iota(jnp.int32, (D, D), 1 if transposed else 0)
    member, row = (n >> 3) & 15, n & 7
    item = 4 * (n >> 7) + (row & 3)
    quarter = (item * 11) >> 5
    up = 48 * quarter + 3 * member + item - 3 * quarter
    return jnp.where(jnp.where(row < 4, up, 192 + 12 * member + item) == o, 1.0, 0.0).astype(BF16)


def place_attend(member, row):
    small = jnp.where(row == 9, 144 + member, 160 + member * 3 + row - 10)
    return jnp.where(row < 9, threes(member, row), jnp.where(row < 13, small, -1))


def members(part, group):
    z, x_lo = group // 2, group % 2
    return [
        slot_of(part, 2 * x_hi + x_lo, y, z, core)
        for y in range(4)
        for core in range(2)
        for x_hi in range(2)
    ]


def bias_map(name, count):
    size, lane = BIASES[name]
    n = lax.broadcasted_iota(jnp.int32, (128, count), 1)
    owner = (n * -(-65536 // size)) >> 16
    k = lax.broadcasted_iota(jnp.int32, (128, count), 0)
    return [jnp.where(hit, 1.0, 0.0).astype(BF16) for hit in (owner == k, n - owner * size + lane == k)]


def bias_row(bias, maps):
    mine, lane = maps
    return jnp.sum(dot(bias, lane) * mine.astype(F32), axis=0, keepdims=True)


def bias_block(row, maps):
    mine, lane = maps
    return dot((mine.astype(F32) * row).astype(BF16), lane, 1, 1)


def weighing(p, at, core, cact_all):
    a, b, c = ORDERS[p]

    def along(c_at, core_at, b_at, a_at):
        spot = {c: c_at, b: b_at, a: a_at}
        return owner_of((spot[0], spot[1], spot[2]), core_at)

    latent = lax.broadcasted_iota(jnp.int32, (64, 128), 0) >> 3
    here = along(latent >> 1, latent & 1, at[b], at[a])
    pick = jnp.where(here == lax.broadcasted_iota(jnp.int32, (64, 128), 1), 1.0, 0.0).astype(BF16)
    cacts = dot(pick, cact_all).astype(BF16)
    n = lax.broadcasted_iota(jnp.int32, (256, D), 0)
    row = n & 15
    section = (row * 11) >> 5
    feature = 3 * along(at[c], core, n >> 6, (n >> 4) & 3) + row - 3 * section
    chosen = jnp.where((feature == lax.broadcasted_iota(jnp.int32, (256, D), 1)) & (row < 9), 1.0, 0.0).astype(BF16)
    weights = dot(chosen, cacts, 1, 1)
    row = lax.broadcasted_iota(jnp.int32, (256, 64), 0) & 15
    return jnp.where((row * 11) >> 5 == (lax.broadcasted_iota(jnp.int32, (256, 64), 1) & 7), weights, 0.0).astype(BF16)


def normalize(v):
    shifted = v - jnp.mean(v, axis=-1, keepdims=True)
    inverse = lax.rsqrt(jnp.mean(shifted * shifted, axis=-1, keepdims=True) + EPS)
    return shifted * inverse, inverse


def denormalize(e, n, inverse):
    return inverse * (
        e - jnp.mean(e, axis=-1, keepdims=True) - n * jnp.mean(e * n, axis=-1, keepdims=True)
    )


def total(v):
    return jnp.sum(v, axis=0, keepdims=True)


def block_kernel(
    tokens, condition, mod, b_mod, att, b_att, out, b_out, up, b_up, down, b_down, cotangent,
    result, token_grad, condition_grad, grad_ff, grad_att, grad_mod,
    held1, held2, pair_vectors, vectors, w_mod, w_att, w_out, w_up, w_down, bias, cact_all,
    d_att, d_out, d_up, d_down, probs_ref,
    packed, chip, ours, ring, joined, row, near, line, ends,
    packed_a, chip_a, ours_a, ring_a, joined_a, row_a, near_a, line_a, ends_a,
    sems,
):
    at, core = place()
    announce(at, core)
    first, second = [Gather(at, core, held, sems.at[i, 0], sems.at[i, 1]) for i, held in enumerate((held1, held2))]
    trade = Moves(at, core, sems.at[2, 0], sems.at[2, 1])
    back = Reduce(at, core, packed, chip, ours, ring, joined, row, near, line, ends, sems.at[3, 0], sems.at[3, 1])
    last = Reduce(
        at, core, packed_a, chip_a, ours_a, ring_a, joined_a, row_a, near_a, line_a, ends_a, sems.at[4, 0], sems.at[4, 1]
    )

    def load(ref, lo, hi):
        return ref[0, :, lo:hi].astype(F32)

    cond = condition[...].astype(F32)
    sigmoid = 1.0 / (1.0 + jnp.exp(-cond))
    cact = (cond * sigmoid).astype(BF16).astype(F32)
    bias_line = jnp.concatenate(
        [ref[...].astype(F32) for ref in (b_mod, b_att, b_out, b_up, b_down)]
        + [jnp.zeros((1, 128 - 42), F32), cact, jnp.zeros((1, 256), F32)],
        axis=1,
    )
    mine = jnp.concatenate(
        [load(mod, 0, 768), load(mod, 768, 1536), load(mod, 1536, 2304), load(att, 0, 768),
         jnp.concatenate([load(att, 768, 1152), load(out, 0, 384)], axis=1), bias_line],
        axis=0,
    ).astype(BF16)
    quarters = jnp.concatenate([load(up, D * i, D * i + D) for i in range(4)], axis=0)
    tall = down[0].astype(F32)
    for p in range(PARTS):
        held1[p, first.own(p)] = mine[:, 256 * p : 256 * p + 256]
        items = slice(4 * p, 4 * p + 4)
        held2[p, second.own(p)] = jnp.concatenate([quarters[items], tall[items]], axis=0).astype(BF16)

    pl.semaphore_wait(pltpu.get_barrier_semaphore(), 10)
    for p in range(PARTS):
        first.first(p)
    for p in range(PARTS):
        second.first(p)

    x = tokens[0].astype(F32)
    g = cotangent[0].astype(F32)
    cact_column = jnp.broadcast_to(cact, (128, D)).T
    n1, inverse1 = normalize(x)
    maps = {name: bias_map(name, 128 * BIASES[name][0]) for name in BIASES}
    first_rows = spread(place_first, 256, False)

    for p in range(PARTS):
        first.second(p)
    for p in range(PARTS):
        second.second(p)
    shuffled, unshuffled, attend_rows = shuffle(False), shuffle(True), spread(place_attend, 208, True)
    for p in range(PARTS):
        first.third(p)
    for p in range(PARTS):
        second.third(p)
    for d in (1, 3, 2):
        for p in range(PARTS):
            first.across(p, d)

    for p in range(PARTS):
        first.complete(p)
        lo = 256 * p
        for group in range(8):
            here = slice(48 * group, 48 * group + 48)
            few = slice(16 * group, 16 * group + 16)
            laid = dot(first_rows, jnp.concatenate([held1[p, s] for s in members(p, group)], axis=0)).astype(BF16)
            for i in range(3):
                w_mod[here, 768 * i + lo : 768 * i + lo + 256] = laid[48 * i : 48 * i + 48]
            w_att[here, lo : lo + 256] = laid[144:192]
            if p == 0:
                w_att[here, 768:1024] = laid[192:240]
                bias[few, :] = laid[240:256, 0:128]
                cact_all[few, 0:128] = laid[240:256, 128:256]
            elif p == 1:
                w_att[here, 1024:1152] = laid[192:240, 0:128]
                w_out[here, 0:128] = laid[192:240, 128:256]
                cact_all[few, 128:384] = laid[240:256]
            else:
                w_out[here, 128:384] = laid[192:240]

    raw_bias = bias[...]
    modulation = jnp.concatenate(
        [total(w_mod[:, 128 * t : 128 * t + 128].astype(F32) * cact_column) for t in range(18)],
        axis=1,
    ) + bias_row(raw_bias, maps["mod"])
    shift1, scale1, gate1, shift2, scale2, gate2 = [
        modulation[:, D * i : D * i + D] for i in range(6)
    ]
    hidden1 = (n1 * (1.0 + scale1) + shift1).astype(BF16)
    b_attend = bias_row(raw_bias, maps["attend"])
    b_full = jnp.concatenate([b_attend[:, :D], jnp.zeros((1, D), F32), b_attend[:, D:]], axis=1)
    triple = (dot(hidden1, w_att[...]) + b_full).astype(BF16)

    def pair(i, which):
        lo = D * which + 128 * i
        return triple[:, lo : lo + 128]

    weights = [weighing(p, at, core, cact_all[...]) for p in range(PARTS)]
    b_output, b_upper, b_lower = [bias_row(raw_bias, maps[name]) for name in ("output", "up", "down")]
    dfeed = (gate2 * g).astype(BF16)
    for d in (1, 3, 2):
        for p in range(PARTS):
            second.across(p, d)

    lane = lax.broadcasted_iota(jnp.int32, (S, 128), 1)
    halves = [lane < 64, lane >= 64]
    nothing = jnp.zeros((S, 128), BF16)
    mixed_pairs = []
    keys_t = []
    for i in range(3):
        q, k, v = pair(i, 0), pair(i, 1), pair(i, 2)
        v_t = v.T
        keys_t.append(k.T)
        mixed_t = []
        for h in range(2):
            scores = dot(k, jnp.where(halves[h], q, nothing), 1, 1) * FACTOR
            e = jnp.exp(scores - jnp.max(scores, axis=0, keepdims=True))
            probs = e * (1.0 / total(e))
            probs_ref[2 * i + h] = probs
            mixed_t.append(dot(v_t[64 * h : 64 * h + 64], probs.astype(BF16)))
        mixed_pairs.append(jnp.concatenate(mixed_t, axis=0).T.astype(BF16))
    mixed = jnp.concatenate(mixed_pairs, axis=1)
    branch = dot(mixed, w_out[...]) + b_output
    middle = x + gate1 * branch
    n2, inverse2 = normalize(middle)
    hidden2 = (n2 * (1.0 + scale2) + shift2).astype(BF16)

    for p in range(PARTS):
        second.complete(p)
    for group in range(8):
        here = slice(48 * group, 48 * group + 48)
        blocks = jnp.concatenate(
            [held2[p, s].astype(F32) for p in range(PARTS) for s in members(p, group)], axis=0
        ).astype(BF16)
        laid = dot(shuffled, blocks).astype(BF16)
        for i in range(4):
            w_up[here, D * i : D * i + D] = laid[48 * i : 48 * i + 48]
        w_down[192 * group : 192 * group + 192, :] = laid[192:384]

    feed = jnp.zeros((S, D), F32)
    dhidden2 = jnp.zeros((S, D), F32)
    db_up = []
    hidden2_t = hidden2.T
    for c in range(4):
        lo = D * c
        upper = dot(hidden2, w_up[:, lo : lo + D]) + b_upper[:, lo : lo + D]
        square = upper * upper
        t = jnp.tanh(0.7978845608028654 * (upper + 0.044715 * (upper * square)))
        half = 0.5 * (1.0 + t)
        activated = (upper * half).astype(BF16)
        slope = half + (0.5 * upper) * (1.0 - t * t) * (
            0.7978845608028654 * (1.0 + 0.134145 * square)
        )
        feed = feed + dot(activated, w_down[lo : lo + D, :])
        dupper = (dot(dfeed, w_down[lo : lo + D, :], 1, 1) * slope).astype(BF16)
        d_down[lo : lo + D, :] = dot(activated.T, dfeed).astype(BF16)
        d_up[:, lo : lo + D] = dot(hidden2_t, dupper).astype(BF16)
        db_up.append(total(dupper.astype(F32)))
        dhidden2 = dhidden2 + dot(dupper, w_up[:, lo : lo + D], 1, 1)
    feed = feed + b_lower
    result[0] = (middle + gate2 * feed).astype(BF16)
    dgate2 = total(g * feed)
    db_down = total(dfeed.astype(F32))
    dscale2, dshift2 = total(dhidden2 * n2), total(dhidden2)
    gmid = g + denormalize(dhidden2 * (1.0 + scale2), n2, inverse2)
    dgate1 = total(gmid * branch)
    dbranch = (gate1 * gmid).astype(BF16)
    d_out[...] = dot(mixed.T, dbranch).astype(BF16)
    db_out = total(dbranch.astype(F32))

    for group in range(8):
        here = slice(48 * group, 48 * group + 48)
        flat = jnp.concatenate(
            [d_up[here, D * i : D * i + D] for i in range(4)] + [d_down[192 * group : 192 * group + 192, :]], axis=0
        )
        laid = dot(unshuffled, flat)
        for p in range(PARTS):
            for m, s in enumerate(members(p, group)):
                packed[p, s] = laid[128 * p + 8 * m : 128 * p + 8 * m + 8].astype(BF16)
    for p in range(PARTS):
        back.across(p)

    dmixed = dot(dbranch, w_out[...], 1, 1).astype(BF16)

    dq, dk, dv = [], [], []
    for i in range(3):
        q, v = pair(i, 0), pair(i, 2)
        dm = dmixed[:, 128 * i : 128 * i + 128]
        dq_t, dk_h, dv_h = [], [], []
        for h in range(2):
            probs = probs_ref[2 * i + h]
            dprobs = dot(v, jnp.where(halves[h], dm, nothing), 1, 1)
            dv_h.append(dot(probs.astype(BF16), dm))
            dscores = (probs * (dprobs - total(probs * dprobs))).astype(BF16)
            dk_h.append(dot(dscores, q))
            dq_t.append(dot(keys_t[i][64 * h : 64 * h + 64], dscores))
        dq.append((jnp.concatenate(dq_t, axis=0).T * FACTOR).astype(BF16))
        dk.append((jnp.where(halves[0], dk_h[0], dk_h[1]) * FACTOR).astype(BF16))
        dv.append(jnp.where(halves[0], dv_h[0], dv_h[1]).astype(BF16))
    for p in range(PARTS):
        back.third(p)
    dtriple = jnp.concatenate(dq + dk + dv, axis=1)
    dhidden1 = dot(dtriple, w_att[...], 1, 1)
    dscale1, dshift1 = total(dhidden1 * n1), total(dhidden1)
    dmod = jnp.concatenate([dshift1, dscale1, dgate1, dshift2, dscale2, dgate2], axis=1)
    sections = jnp.concatenate([dmod[:, 768 * i : 768 * i + 768] for i in range(3)] + [jnp.zeros((5, 768), F32)], axis=0)
    for p in range(PARTS):
        pair_vectors[core, p] = sections[:, 256 * p : 256 * p + 256]
    trade.start(0, 0, 0, pair_vectors.at[core], pair_vectors.at[core], None, 0)
    d_att[...] = dot(hidden1.T, dtriple).astype(BF16)
    sums = total(dtriple.astype(F32))
    db_att = jnp.concatenate([sums[:, :D], sums[:, 2 * D :]], axis=1)
    d_bias = (
        bias_block(dmod, maps["mod"])
        + bias_block(db_att, maps["attend"])
        + bias_block(db_out, maps["output"])
        + bias_block(jnp.concatenate(db_up, axis=1), maps["up"])
        + bias_block(db_down, maps["down"])
    ).astype(BF16)
    for group in range(8):
        here = slice(48 * group, 48 * group + 48)
        biases = jnp.concatenate([d_bias[16 * group : 16 * group + 16], jnp.zeros((16, 256), BF16)], axis=1)
        flat = jnp.concatenate([d_att[here, 0:384], d_att[here, 384:768], d_att[here, 768:1152], biases, d_out[here, :]], axis=0)
        laid = dot(attend_rows, flat).astype(BF16)
        for p in range(PARTS):
            for m, s in enumerate(members(p, group)):
                packed_a[p, s] = laid[16 * m : 16 * m + 16, 128 * p : 128 * p + 128]
    for p in range(PARTS):
        last.across(p)

    trade.arrived(0, 0, (0,))
    for p in range(PARTS):
        c = ORDERS[p][2]
        for d in (1, 3, 2):
            trade.start(1, p, d, pair_vectors.at[:, p], vectors.at[p, at[c]], c, d)
        vectors[p, at[c]] = pair_vectors[:, p]
    for p in range(PARTS):
        last.third(p)
    for p in range(PARTS):
        back.second(p)
    token_grad[0] = gmid + denormalize(dhidden1 * (1.0 + scale1), n1, inverse1)
    dcact = jnp.zeros((D, 128), F32)
    for t in range(18):
        here = slice(128 * t, 128 * t + 128)
        dcact = dcact + w_mod[:, here].astype(F32) * dmod[:, here]
    condition_grad[...] = total(dcact.T) * (sigmoid * (1.0 + cond * (1.0 - sigmoid)))

    for p in range(PARTS):
        trade.arrived(1, p, (1, 3, 2))
    d_mod = [dot(weights[p], vectors[p].reshape(64, 256).astype(BF16)).astype(BF16) for p in range(PARTS)]
    for p in range(PARTS):
        last.second(p, d_mod[p].reshape(16, 16, 256))
    for p in range(PARTS):
        back.first(p)
    for p in range(PARTS):
        last.first(p)
    for p in range(PARTS):
        grad_ff[8 * p : 8 * p + 8, :] = back.total(p)
    for p in range(PARTS):
        summed = last.total(p)
        grad_att[:, 128 * p : 128 * p + 128] = summed[:, 0:128]
        grad_mod[:, 256 * p : 256 * p + 256] = summed[:, 128:384]
    for moves in (first, second, trade, back, last):
        moves.sent()


def unpack_kernel(
    result_in, token_in, condition_in, ff, attend, modulation,
    result, token_grad, condition_grad, mod, b_mod, att, b_att, out, b_out, up, b_up, down, b_down,
):
    result[...] = result_in[...]
    token_grad[...] = token_in[...]
    condition_grad[...] = condition_in[...]
    for i in range(3):
        mod[:, 0, 768 * i : 768 * i + 768] = modulation[3 * i : 3 * i + 3, :]
        att[:, 0, D * i : D * i + D] = attend[3 * i : 3 * i + 3, :]
    for i in range(12):
        lo = 8 * (i // 4) + i % 4
        up[i % 3, :, D * (i // 3) : D * (i // 3) + D] = ff[lo : lo + 1, :]
        down[i] = ff[lo + 4 : lo + 5, :]
    out[:, 0, :] = attend[10:13, :]
    for ref, name in ((b_mod, "mod"), (b_att, "attend"), (b_out, "output"), (b_up, "up"), (b_down, "down")):
        size, lane = BIASES[name]
        ref[...] = attend[9:10, lane : lane + size]


def whole(count):
    return [pl.BlockSpec(memory_space=pltpu.VMEM)] * count


def shape(*dims, dtype=BF16):
    return jax.ShapeDtypeStruct(dims, dtype)


def reduce_scratch(tall, wide, wider):
    return [
        pltpu.VMEM((PARTS, 128, tall, wide), BF16),
        pltpu.VMEM((PARTS, 64, tall, wide), BF16),
        pltpu.VMEM((PARTS, 64, tall, wide), BF16),
        pltpu.VMEM((PARTS, 3, 16, tall, wide), BF16),
        pltpu.VMEM((PARTS, 16, tall, wider), BF16),
        pltpu.VMEM((PARTS, 3, 4, tall, wider), BF16),
        pltpu.VMEM((PARTS, 4, tall, wider), F32),
        pltpu.VMEM((PARTS, 4, tall, wider), BF16),
        pltpu.VMEM((PARTS, 3, tall, wider), BF16),
    ]


def local(*args):
    outs = [
        shape(1, S, D), shape(1, S, D, dtype=F32), shape(1, D, dtype=F32),
    ]
    computed = pl.pallas_call(
        block_kernel,
        out_shape=outs + [shape(24, D, dtype=F32), shape(16, D, dtype=F32), shape(16, 768, dtype=F32)],
        in_specs=whole(13),
        out_specs=whole(6),
        scratch_shapes=[
            pltpu.VMEM((PARTS, 128, 16, 256), BF16),
            pltpu.VMEM((PARTS, 128, 8, D), BF16),
            pltpu.VMEM((2, PARTS, 8, 256), F32),
            pltpu.VMEM((PARTS, 4, 2, 8, 256), F32),
            pltpu.VMEM((D, 6 * D), BF16), pltpu.VMEM((D, 3 * D), BF16), pltpu.VMEM((D, D), BF16),
            pltpu.VMEM((D, FF), BF16), pltpu.VMEM((FF, D), BF16), pltpu.VMEM((128, 128), BF16), pltpu.VMEM((128, D), BF16),
            pltpu.VMEM((D, 3 * D), BF16), pltpu.VMEM((D, D), BF16),
            pltpu.VMEM((D, FF), BF16), pltpu.VMEM((FF, D), BF16), pltpu.VMEM((6, S, S), F32),
            *reduce_scratch(8, D, D),
            *reduce_scratch(16, 128, D),
            pltpu.SemaphoreType.DMA((5, 2, 4, PARTS, 4)),
        ],
        compiler_params=pltpu.CompilerParams(
            collective_id=0, has_side_effects=True, vmem_limit_bytes=VMEM_LIMIT
        ),
    )(*args)
    grads = [
        shape(3, 1, 6 * D, dtype=F32), shape(1, 18, dtype=F32), shape(3, 1, 3 * D, dtype=F32),
        shape(1, 6, dtype=F32), shape(3, 1, D, dtype=F32), shape(1, 3, dtype=F32),
        shape(3, 1, FF, dtype=F32), shape(1, 12, dtype=F32), shape(12, 1, D, dtype=F32), shape(1, 3, dtype=F32),
    ]
    final = pl.pallas_call(
        unpack_kernel, out_shape=outs + grads, in_specs=whole(6), out_specs=whole(13)
    )(*computed)
    return tuple(
        jnp.swapaxes(item, 0, 1) if i >= 3 and item.ndim == 3 else item for i, item in enumerate(final)
    )


def solution(mesh):
    latents = P(("dp", "fsdp"), None, None)
    rows = P(None, ("dp", "fsdp"), None)
    entries = P(None, ("dp", "fsdp"))
    weights = (rows, entries) * 5
    return jax.shard_map(
        local,
        mesh=mesh,
        in_specs=(latents, P(("dp", "fsdp"), None), *weights, latents),
        out_specs=(latents, latents, P(("dp", "fsdp"), None), *weights),
        check_vma=False,
    )
```

```python
import jax
import jax.numpy as jnp
from jax import lax
from jax.experimental import pallas as pl
from jax.experimental.pallas import tpu as pltpu
from jax.sharding import PartitionSpec as P

MESH = pl.DeviceIdType.MESH
F32 = jnp.float32
BF16 = jnp.bfloat16
EPS = 1e-06
HEAD = 64
D = 384
FF = 1536
S = 256
FACTOR = HEAD ** (-0.5)
VMEM_LIMIT = 60 * 1024 * 1024

PARTS = 3
ORDERS = ((0, 1, 2), (1, 2, 0), (2, 0, 1))
BIASES = {"mod": (18, 0), "attend": (6, 18), "output": (3, 24), "up": (12, 27), "down": (3, 39)}


def dot(a, b, ca=1, cb=0):
    return lax.dot_general(a, b, (((ca,), (cb,)), ((), ())), preferred_element_type=F32)


def place():
    dp, fsdp = lax.axis_index("dp"), lax.axis_index("fsdp")
    core = lax.rem(dp, 2)
    y = lax.rem(lax.div(dp, 2), 4)
    x = lax.rem(lax.div(dp, 8), 2) + 2 * fsdp
    return (x, y, lax.div(dp, 16)), core


def device(at, core):
    x, y, z = at
    return (z * 16 + lax.rem(x, 2) * 8 + y * 2 + core, lax.div(x, 2))


def owner_of(at, core):
    x, y, z = at
    return z * 32 + (x & 1) * 16 + y * 4 + core * 2 + (x >> 1)


def moved(at, axis, by):
    return tuple(lax.rem(c + by, 4) if i == axis else c for i, c in enumerate(at))


def slot_of(part, x, y, z, core):
    at = (x, y, z)
    a, b, c = ORDERS[part]
    return ((core * 4 + at[c]) * 4 + at[b]) * 4 + at[a]


def announce(at, core):
    barrier = pltpu.get_barrier_semaphore()
    for axis in range(3):
        for by in range(1, 4):
            pl.semaphore_signal(
                barrier, inc=1, device_id=device(moved(at, axis, by), core), device_id_type=MESH
            )
    pl.semaphore_signal(barrier, inc=1, device_id=device(at, 1 - core), device_id_type=MESH)


class Moves:
    def __init__(self, at, core, send, recv):
        self.at, self.core, self.send, self.recv = at, core, send, recv
        self.copies = {}

    def start(self, stage, p, k, src, dst, axis, by):
        to = device(self.at, 1 - self.core) if axis is None else device(moved(self.at, axis, by), self.core)
        copy = pltpu.make_async_remote_copy(
            src_ref=src, dst_ref=dst, send_sem=self.send.at[stage, p, k], recv_sem=self.recv.at[stage, p, k],
            device_id=to, device_id_type=MESH,
        )
        copy.start()
        self.copies[stage, p, k] = copy

    def arrived(self, stage, p, ks):
        for k in ks:
            self.copies[stage, p, k].wait_recv()

    def sent(self):
        for copy in self.copies.values():
            copy.wait_send()


class Gather(Moves):
    def __init__(self, at, core, held, send, recv):
        super().__init__(at, core, send, recv)
        self.held = held

    def own(self, p):
        return slot_of(p, *self.at, self.core)

    def first(self, p):
        block = self.held.at[p, pl.ds(self.own(p), 1)]
        for d in (1, 3, 2):
            self.start(0, p, d, block, block, ORDERS[p][0], d)

    def second(self, p):
        self.arrived(0, p, (1, 3, 2))
        _, b, c = ORDERS[p]
        block = self.held.at[p, pl.ds(((self.core * 4 + self.at[c]) * 4 + self.at[b]) * 4, 4)]
        for d in (1, 3, 2):
            self.start(1, p, d, block, block, b, d)

    def plane(self, p, by):
        lo = (self.core * 4 + lax.rem(self.at[ORDERS[p][2]] + by, 4)) * 16
        return self.held.at[p, pl.ds(lo, 16)]

    def third(self, p):
        self.arrived(1, p, (1, 3, 2))
        block = self.plane(p, 0)
        for d in (1, 3, 2):
            self.start(2, p, d, block, block, ORDERS[p][2], d)
        self.start(3, p, 0, block, block, None, 0)

    def across(self, p, d):
        self.arrived(2, p, (d,))
        block = self.plane(p, 4 - d)
        self.start(3, p, d, block, block, None, 0)

    def complete(self, p):
        self.arrived(3, p, range(4))


def add(*blocks):
    out = blocks[0].astype(F32)
    for block in blocks[1:]:
        out = out + block.astype(F32)
    return out


class Reduce(Moves):
    def __init__(self, at, core, packed, chip, ours, ring, joined, row, near, line, ends, send, recv):
        super().__init__(at, core, send, recv)
        self.packed, self.chip, self.ours, self.ring, self.joined = packed, chip, ours, ring, joined
        self.row, self.near, self.line, self.ends = row, near, line, ends

    def chunk(self, p, by):
        return lax.rem(self.at[ORDERS[p][2]] + by, 4) * 16

    def across(self, p):
        self.start(0, p, 0, self.packed.at[p, pl.ds((1 - self.core) * 64, 64)], self.chip.at[p], None, 0)

    def third(self, p):
        self.arrived(0, p, (0,))
        for by in (2, 1, 3, 0):
            lo = self.chunk(p, by)
            here = pl.ds(lo, 16)
            self.ours[p, here] = self.packed[p, pl.ds(self.core * 64 + lo, 16)] + self.chip[p, here]
            if by:
                self.start(1, p, by, self.ours.at[p, here], self.ring.at[p, by - 1], ORDERS[p][2], by)

    def second(self, p, more=None):
        self.arrived(1, p, (1, 3, 2))
        ring = self.ring
        wide = ring.shape[-1]
        summed = add(self.ours[p, pl.ds(self.chunk(p, 0), 16)], ring[p, 0], ring[p, 1], ring[p, 2]).astype(BF16)
        self.joined[p, :, :, 0:wide] = summed
        if more is not None:
            self.joined[p, :, :, wide:] = more
        b = ORDERS[p][1]
        for d in (2, 1, 3):
            src = self.joined.at[p, pl.ds(lax.rem(self.at[b] + d, 4) * 4, 4)]
            self.start(2, p, d, src, self.row.at[p, d - 1], b, d)

    def first(self, p):
        self.arrived(2, p, (1, 3, 2))
        a, b, _ = ORDERS[p]
        row = self.row
        self.near[p] = add(self.joined[p, pl.ds(self.at[b] * 4, 4)], row[p, 0], row[p, 1], row[p, 2])
        self.line[p] = self.near[p].astype(BF16)
        for d in (2, 1, 3):
            src = self.line.at[p, pl.ds(lax.rem(self.at[a] + d, 4), 1)]
            self.start(3, p, d, src, self.ends.at[p, pl.ds(d - 1, 1)], a, d)

    def total(self, p):
        self.arrived(3, p, (1, 3, 2))
        ends = self.ends
        return add(self.near[p, self.at[ORDERS[p][0]]], ends[p, 0], ends[p, 1], ends[p, 2])


def spread(place_of, count, transposed):
    shape = (256, count) if transposed else (count, 256)
    n = lax.broadcasted_iota(jnp.int32, shape, 0 if transposed else 1)
    o = lax.broadcasted_iota(jnp.int32, shape, 1 if transposed else 0)
    return jnp.where(place_of(n >> 4, n & 15) == o, 1.0, 0.0).astype(BF16)


def threes(member, row):
    section = (row * 11) >> 5
    return section * 48 + member * 3 + (row - 3 * section)


def place_first(member, row):
    return jnp.where(row == 15, 240 + member, threes(member, row))


def shuffle(transposed):
    n = lax.broadcasted_iota(jnp.int32, (D, D), 0 if transposed else 1)
    o = lax.broadcasted_iota(jnp.int32, (D, D), 1 if transposed else 0)
    member, row = (n >> 3) & 15, n & 7
    item = 4 * (n >> 7) + (row & 3)
    quarter = (item * 11) >> 5
    up = 48 * quarter + 3 * member + item - 3 * quarter
    return jnp.where(jnp.where(row < 4, up, 192 + 12 * member + item) == o, 1.0, 0.0).astype(BF16)


def place_attend(member, row):
    small = jnp.where(row == 9, 144 + member, 160 + member * 3 + row - 10)
    return jnp.where(row < 9, threes(member, row), jnp.where(row < 13, small, -1))


def members(part, group):
    z, x_lo = group // 2, group % 2
    return [
        slot_of(part, 2 * x_hi + x_lo, y, z, core)
        for y in range(4)
        for core in range(2)
        for x_hi in range(2)
    ]


def bias_map(name, count):
    size, lane = BIASES[name]
    n = lax.broadcasted_iota(jnp.int32, (128, count), 1)
    owner = (n * -(-65536 // size)) >> 16
    k = lax.broadcasted_iota(jnp.int32, (128, count), 0)
    return [jnp.where(hit, 1.0, 0.0).astype(BF16) for hit in (owner == k, n - owner * size + lane == k)]


def bias_row(bias, maps):
    mine, lane = maps
    return jnp.sum(dot(bias, lane) * mine.astype(F32), axis=0, keepdims=True)


def bias_block(row, maps):
    mine, lane = maps
    return dot((mine.astype(F32) * row).astype(BF16), lane, 1, 1)


def weighing(p, at, core, cact_all):
    a, b, c = ORDERS[p]

    def along(c_at, core_at, b_at, a_at):
        spot = {c: c_at, b: b_at, a: a_at}
        return owner_of((spot[0], spot[1], spot[2]), core_at)

    latent = lax.broadcasted_iota(jnp.int32, (64, 128), 0) >> 3
    here = along(latent >> 1, latent & 1, at[b], at[a])
    pick = jnp.where(here == lax.broadcasted_iota(jnp.int32, (64, 128), 1), 1.0, 0.0).astype(BF16)
    cacts = dot(pick, cact_all).astype(BF16)
    n = lax.broadcasted_iota(jnp.int32, (256, D), 0)
    row = n & 15
    section = (row * 11) >> 5
    feature = 3 * along(at[c], core, n >> 6, (n >> 4) & 3) + row - 3 * section
    chosen = jnp.where((feature == lax.broadcasted_iota(jnp.int32, (256, D), 1)) & (row < 9), 1.0, 0.0).astype(BF16)
    weights = dot(chosen, cacts, 1, 1)
    row = lax.broadcasted_iota(jnp.int32, (256, 64), 0) & 15
    return jnp.where((row * 11) >> 5 == (lax.broadcasted_iota(jnp.int32, (256, 64), 1) & 7), weights, 0.0).astype(BF16)


def normalize(v):
    shifted = v - jnp.mean(v, axis=-1, keepdims=True)
    inverse = lax.rsqrt(jnp.mean(shifted * shifted, axis=-1, keepdims=True) + EPS)
    return shifted * inverse, inverse


def denormalize(e, n, inverse):
    return inverse * (
        e - jnp.mean(e, axis=-1, keepdims=True) - n * jnp.mean(e * n, axis=-1, keepdims=True)
    )


def total(v):
    return jnp.sum(v, axis=0, keepdims=True)


def block_kernel(
    tokens, condition, mod, b_mod, att, b_att, out, b_out, up, b_up, down, b_down, cotangent,
    result, token_grad, condition_grad, grad_ff, grad_att, grad_mod,
    held1, held2, pair_vectors, vectors, w_mod, w_att, w_out, w_up, w_down, bias, cact_all,
    d_att, d_out, d_up, d_down, probs_ref,
    packed, chip, ours, ring, joined, row, near, line, ends,
    packed_a, chip_a, ours_a, ring_a, joined_a, row_a, near_a, line_a, ends_a,
    sems,
):
    at, core = place()
    announce(at, core)
    first, second = [Gather(at, core, held, sems.at[i, 0], sems.at[i, 1]) for i, held in enumerate((held1, held2))]
    trade = Moves(at, core, sems.at[2, 0], sems.at[2, 1])
    back = Reduce(at, core, packed, chip, ours, ring, joined, row, near, line, ends, sems.at[3, 0], sems.at[3, 1])
    last = Reduce(
        at, core, packed_a, chip_a, ours_a, ring_a, joined_a, row_a, near_a, line_a, ends_a, sems.at[4, 0], sems.at[4, 1]
    )

    def load(ref, lo, hi):
        return ref[0, :, lo:hi].astype(F32)

    cond = condition[...].astype(F32)
    sigmoid = 1.0 / (1.0 + jnp.exp(-cond))
    cact = (cond * sigmoid).astype(BF16).astype(F32)
    bias_line = jnp.concatenate(
        [ref[...].astype(F32) for ref in (b_mod, b_att, b_out, b_up, b_down)]
        + [jnp.zeros((1, 128 - 42), F32), cact, jnp.zeros((1, 256), F32)],
        axis=1,
    )
    mine = jnp.concatenate(
        [load(mod, 0, 768), load(mod, 768, 1536), load(mod, 1536, 2304), load(att, 0, 768),
         jnp.concatenate([load(att, 768, 1152), load(out, 0, 384)], axis=1), bias_line],
        axis=0,
    ).astype(BF16)
    quarters = jnp.concatenate([load(up, D * i, D * i + D) for i in range(4)], axis=0)
    tall = down[0].astype(F32)
    for p in range(PARTS):
        held1[p, first.own(p)] = mine[:, 256 * p : 256 * p + 256]
        items = slice(4 * p, 4 * p + 4)
        held2[p, second.own(p)] = jnp.concatenate([quarters[items], tall[items]], axis=0).astype(BF16)

    pl.semaphore_wait(pltpu.get_barrier_semaphore(), 10)
    for p in range(PARTS):
        first.first(p)
    for p in range(PARTS):
        second.first(p)

    x = tokens[0].astype(F32)
    g = cotangent[0].astype(F32)
    cact_column = jnp.broadcast_to(cact, (128, D)).T
    n1, inverse1 = normalize(x)
    maps = {name: bias_map(name, 128 * BIASES[name][0]) for name in BIASES}
    first_rows = spread(place_first, 256, False)

    for p in range(PARTS):
        first.second(p)
    for p in range(PARTS):
        second.second(p)
    shuffled, unshuffled, attend_rows = shuffle(False), shuffle(True), spread(place_attend, 208, True)
    for p in range(PARTS):
        first.third(p)
    for p in range(PARTS):
        second.third(p)
    for d in (1, 3, 2):
        for p in range(PARTS):
            first.across(p, d)

    for p in range(PARTS):
        first.complete(p)
        lo = 256 * p
        for group in range(8):
            here = slice(48 * group, 48 * group + 48)
            few = slice(16 * group, 16 * group + 16)
            laid = dot(first_rows, jnp.concatenate([held1[p, s] for s in members(p, group)], axis=0)).astype(BF16)
            for i in range(3):
                w_mod[here, 768 * i + lo : 768 * i + lo + 256] = laid[48 * i : 48 * i + 48]
            w_att[here, lo : lo + 256] = laid[144:192]
            if p == 0:
                w_att[here, 768:1024] = laid[192:240]
                bias[few, :] = laid[240:256, 0:128]
                cact_all[few, 0:128] = laid[240:256, 128:256]
            elif p == 1:
                w_att[here, 1024:1152] = laid[192:240, 0:128]
                w_out[here, 0:128] = laid[192:240, 128:256]
                cact_all[few, 128:384] = laid[240:256]
            else:
                w_out[here, 128:384] = laid[192:240]

    raw_bias = bias[...]
    modulation = jnp.concatenate(
        [total(w_mod[:, 128 * t : 128 * t + 128].astype(F32) * cact_column) for t in range(18)],
        axis=1,
    ) + bias_row(raw_bias, maps["mod"])
    shift1, scale1, gate1, shift2, scale2, gate2 = [
        modulation[:, D * i : D * i + D] for i in range(6)
    ]
    hidden1 = (n1 * (1.0 + scale1) + shift1).astype(BF16)
    b_attend = bias_row(raw_bias, maps["attend"])
    b_full = jnp.concatenate([b_attend[:, :D], jnp.zeros((1, D), F32), b_attend[:, D:]], axis=1)
    triple = (dot(hidden1, w_att[...]) + b_full).astype(BF16)

    def pair(i, which):
        lo = D * which + 128 * i
        return triple[:, lo : lo + 128]

    weights = [weighing(p, at, core, cact_all[...]) for p in range(PARTS)]
    b_output, b_upper, b_lower = [bias_row(raw_bias, maps[name]) for name in ("output", "up", "down")]
    dfeed = (gate2 * g).astype(BF16)
    for d in (1, 3, 2):
        for p in range(PARTS):
            second.across(p, d)

    lane = lax.broadcasted_iota(jnp.int32, (S, 128), 1)
    halves = [lane < 64, lane >= 64]
    nothing = jnp.zeros((S, 128), BF16)
    mixed_pairs = []
    keys_t = []
    for i in range(3):
        q, k, v = pair(i, 0), pair(i, 1), pair(i, 2)
        v_t = v.T
        keys_t.append(k.T)
        mixed_t = []
        for h in range(2):
            scores = dot(k, jnp.where(halves[h], q, nothing), 1, 1) * FACTOR
            e = jnp.exp(scores - jnp.max(scores, axis=0, keepdims=True))
            probs = e * (1.0 / total(e))
            probs_ref[2 * i + h] = probs
            mixed_t.append(dot(v_t[64 * h : 64 * h + 64], probs.astype(BF16)))
        mixed_pairs.append(jnp.concatenate(mixed_t, axis=0).T.astype(BF16))
    mixed = jnp.concatenate(mixed_pairs, axis=1)
    branch = dot(mixed, w_out[...]) + b_output
    middle = x + gate1 * branch
    n2, inverse2 = normalize(middle)
    hidden2 = (n2 * (1.0 + scale2) + shift2).astype(BF16)

    for p in range(PARTS):
        second.complete(p)
    for group in range(8):
        here = slice(48 * group, 48 * group + 48)
        blocks = jnp.concatenate(
            [held2[p, s].astype(F32) for p in range(PARTS) for s in members(p, group)], axis=0
        ).astype(BF16)
        laid = dot(shuffled, blocks).astype(BF16)
        for i in range(4):
            w_up[here, D * i : D * i + D] = laid[48 * i : 48 * i + 48]
        w_down[192 * group : 192 * group + 192, :] = laid[192:384]

    feed = jnp.zeros((S, D), F32)
    dhidden2 = jnp.zeros((S, D), F32)
    db_up = []
    hidden2_t = hidden2.T
    for c in range(2):
        lo = 768 * c
        upper = dot(hidden2, w_up[:, lo : lo + 768]) + b_upper[:, lo : lo + 768]
        square = upper * upper
        t = jnp.tanh(0.7978845608028654 * (upper + 0.044715 * (upper * square)))
        half = 0.5 * (1.0 + t)
        activated = (upper * half).astype(BF16)
        slope = half + (0.5 * upper) * (1.0 - t * t) * (
            0.7978845608028654 * (1.0 + 0.134145 * square)
        )
        feed = feed + dot(activated, w_down[lo : lo + 768, :])
        dupper = (dot(dfeed, w_down[lo : lo + 768, :], 1, 1) * slope).astype(BF16)
        d_down[lo : lo + 768, :] = dot(activated.T, dfeed).astype(BF16)
        d_up[:, lo : lo + 768] = dot(hidden2_t, dupper).astype(BF16)
        db_up.append(total(dupper.astype(F32)))
        dhidden2 = dhidden2 + dot(dupper, w_up[:, lo : lo + 768], 1, 1)
    feed = feed + b_lower
    result[0] = (middle + gate2 * feed).astype(BF16)
    dgate2 = total(g * feed)
    db_down = total(dfeed.astype(F32))
    dscale2, dshift2 = total(dhidden2 * n2), total(dhidden2)
    gmid = g + denormalize(dhidden2 * (1.0 + scale2), n2, inverse2)
    dgate1 = total(gmid * branch)
    dbranch = (gate1 * gmid).astype(BF16)
    d_out[...] = dot(mixed.T, dbranch).astype(BF16)
    db_out = total(dbranch.astype(F32))

    for group in range(8):
        here = slice(48 * group, 48 * group + 48)
        flat = jnp.concatenate(
            [d_up[here, D * i : D * i + D] for i in range(4)] + [d_down[192 * group : 192 * group + 192, :]], axis=0
        )
        laid = dot(unshuffled, flat)
        for p in range(PARTS):
            for m, s in enumerate(members(p, group)):
                packed[p, s] = laid[128 * p + 8 * m : 128 * p + 8 * m + 8].astype(BF16)
    for p in range(PARTS):
        back.across(p)

    dmixed = dot(dbranch, w_out[...], 1, 1).astype(BF16)

    dq, dk, dv = [], [], []
    for i in range(3):
        q, v = pair(i, 0), pair(i, 2)
        dm = dmixed[:, 128 * i : 128 * i + 128]
        dq_t, dk_h, dv_h = [], [], []
        for h in range(2):
            probs = probs_ref[2 * i + h]
            dprobs = dot(v, jnp.where(halves[h], dm, nothing), 1, 1)
            dv_h.append(dot(probs.astype(BF16), dm))
            dscores = (probs * (dprobs - total(probs * dprobs))).astype(BF16)
            dk_h.append(dot(dscores, q))
            dq_t.append(dot(keys_t[i][64 * h : 64 * h + 64], dscores))
        dq.append((jnp.concatenate(dq_t, axis=0).T * FACTOR).astype(BF16))
        dk.append((jnp.where(halves[0], dk_h[0], dk_h[1]) * FACTOR).astype(BF16))
        dv.append(jnp.where(halves[0], dv_h[0], dv_h[1]).astype(BF16))
    for p in range(PARTS):
        back.third(p)
    dtriple = jnp.concatenate(dq + dk + dv, axis=1)
    dhidden1 = dot(dtriple, w_att[...], 1, 1)
    dscale1, dshift1 = total(dhidden1 * n1), total(dhidden1)
    dmod = jnp.concatenate([dshift1, dscale1, dgate1, dshift2, dscale2, dgate2], axis=1)
    sections = jnp.concatenate([dmod[:, 768 * i : 768 * i + 768] for i in range(3)] + [jnp.zeros((5, 768), F32)], axis=0)
    for p in range(PARTS):
        pair_vectors[core, p] = sections[:, 256 * p : 256 * p + 256]
    trade.start(0, 0, 0, pair_vectors.at[core], pair_vectors.at[core], None, 0)
    d_att[...] = dot(hidden1.T, dtriple).astype(BF16)
    sums = total(dtriple.astype(F32))
    db_att = jnp.concatenate([sums[:, :D], sums[:, 2 * D :]], axis=1)
    d_bias = (
        bias_block(dmod, maps["mod"])
        + bias_block(db_att, maps["attend"])
        + bias_block(db_out, maps["output"])
        + bias_block(jnp.concatenate(db_up, axis=1), maps["up"])
        + bias_block(db_down, maps["down"])
    ).astype(BF16)
    for group in range(8):
        here = slice(48 * group, 48 * group + 48)
        biases = jnp.concatenate([d_bias[16 * group : 16 * group + 16], jnp.zeros((16, 256), BF16)], axis=1)
        flat = jnp.concatenate([d_att[here, 0:384], d_att[here, 384:768], d_att[here, 768:1152], biases, d_out[here, :]], axis=0)
        laid = dot(attend_rows, flat).astype(BF16)
        for p in range(PARTS):
            for m, s in enumerate(members(p, group)):
                packed_a[p, s] = laid[16 * m : 16 * m + 16, 128 * p : 128 * p + 128]
    for p in range(PARTS):
        last.across(p)

    trade.arrived(0, 0, (0,))
    for p in range(PARTS):
        c = ORDERS[p][2]
        for d in (1, 3, 2):
            trade.start(1, p, d, pair_vectors.at[:, p], vectors.at[p, at[c]], c, d)
        vectors[p, at[c]] = pair_vectors[:, p]
    for p in range(PARTS):
        last.third(p)
    for p in range(PARTS):
        back.second(p)
    token_grad[0] = gmid + denormalize(dhidden1 * (1.0 + scale1), n1, inverse1)
    dcact = jnp.zeros((D, 128), F32)
    for t in range(18):
        here = slice(128 * t, 128 * t + 128)
        dcact = dcact + w_mod[:, here].astype(F32) * dmod[:, here]
    condition_grad[...] = total(dcact.T) * (sigmoid * (1.0 + cond * (1.0 - sigmoid)))

    for p in range(PARTS):
        trade.arrived(1, p, (1, 3, 2))
    d_mod = [dot(weights[p], vectors[p].reshape(64, 256).astype(BF16)).astype(BF16) for p in range(PARTS)]
    for p in range(PARTS):
        last.second(p, d_mod[p].reshape(16, 16, 256))
    for p in range(PARTS):
        back.first(p)
    for p in range(PARTS):
        last.first(p)
    for p in range(PARTS):
        grad_ff[8 * p : 8 * p + 8, :] = back.total(p)
    for p in range(PARTS):
        summed = last.total(p)
        grad_att[:, 128 * p : 128 * p + 128] = summed[:, 0:128]
        grad_mod[:, 256 * p : 256 * p + 256] = summed[:, 128:384]
    for moves in (first, second, trade, back, last):
        moves.sent()


def unpack_kernel(
    result_in, token_in, condition_in, ff, attend, modulation,
    result, token_grad, condition_grad, mod, b_mod, att, b_att, out, b_out, up, b_up, down, b_down,
):
    result[...] = result_in[...]
    token_grad[...] = token_in[...]
    condition_grad[...] = condition_in[...]
    for i in range(3):
        mod[:, 0, 768 * i : 768 * i + 768] = modulation[3 * i : 3 * i + 3, :]
        att[:, 0, D * i : D * i + D] = attend[3 * i : 3 * i + 3, :]
    for i in range(12):
        lo = 8 * (i // 4) + i % 4
        up[i % 3, :, D * (i // 3) : D * (i // 3) + D] = ff[lo : lo + 1, :]
        down[i] = ff[lo + 4 : lo + 5, :]
    out[:, 0, :] = attend[10:13, :]
    for ref, name in ((b_mod, "mod"), (b_att, "attend"), (b_out, "output"), (b_up, "up"), (b_down, "down")):
        size, lane = BIASES[name]
        ref[...] = attend[9:10, lane : lane + size]


def whole(count):
    return [pl.BlockSpec(memory_space=pltpu.VMEM)] * count


def shape(*dims, dtype=BF16):
    return jax.ShapeDtypeStruct(dims, dtype)


def reduce_scratch(tall, wide, wider):
    return [
        pltpu.VMEM((PARTS, 128, tall, wide), BF16),
        pltpu.VMEM((PARTS, 64, tall, wide), BF16),
        pltpu.VMEM((PARTS, 64, tall, wide), BF16),
        pltpu.VMEM((PARTS, 3, 16, tall, wide), BF16),
        pltpu.VMEM((PARTS, 16, tall, wider), BF16),
        pltpu.VMEM((PARTS, 3, 4, tall, wider), BF16),
        pltpu.VMEM((PARTS, 4, tall, wider), F32),
        pltpu.VMEM((PARTS, 4, tall, wider), BF16),
        pltpu.VMEM((PARTS, 3, tall, wider), BF16),
    ]


def local(*args):
    outs = [
        shape(1, S, D), shape(1, S, D, dtype=F32), shape(1, D, dtype=F32),
    ]
    computed = pl.pallas_call(
        block_kernel,
        out_shape=outs + [shape(24, D, dtype=F32), shape(16, D, dtype=F32), shape(16, 768, dtype=F32)],
        in_specs=whole(13),
        out_specs=whole(6),
        scratch_shapes=[
            pltpu.VMEM((PARTS, 128, 16, 256), BF16),
            pltpu.VMEM((PARTS, 128, 8, D), BF16),
            pltpu.VMEM((2, PARTS, 8, 256), F32),
            pltpu.VMEM((PARTS, 4, 2, 8, 256), F32),
            pltpu.VMEM((D, 6 * D), BF16), pltpu.VMEM((D, 3 * D), BF16), pltpu.VMEM((D, D), BF16),
            pltpu.VMEM((D, FF), BF16), pltpu.VMEM((FF, D), BF16), pltpu.VMEM((128, 128), BF16), pltpu.VMEM((128, D), BF16),
            pltpu.VMEM((D, 3 * D), BF16), pltpu.VMEM((D, D), BF16),
            pltpu.VMEM((D, FF), BF16), pltpu.VMEM((FF, D), BF16), pltpu.VMEM((6, S, S), F32),
            *reduce_scratch(8, D, D),
            *reduce_scratch(16, 128, D),
            pltpu.SemaphoreType.DMA((5, 2, 4, PARTS, 4)),
        ],
        compiler_params=pltpu.CompilerParams(
            collective_id=0, has_side_effects=True, vmem_limit_bytes=VMEM_LIMIT
        ),
    )(*args)
    grads = [
        shape(3, 1, 6 * D, dtype=F32), shape(1, 18, dtype=F32), shape(3, 1, 3 * D, dtype=F32),
        shape(1, 6, dtype=F32), shape(3, 1, D, dtype=F32), shape(1, 3, dtype=F32),
        shape(3, 1, FF, dtype=F32), shape(1, 12, dtype=F32), shape(12, 1, D, dtype=F32), shape(1, 3, dtype=F32),
    ]
    final = pl.pallas_call(
        unpack_kernel, out_shape=outs + grads, in_specs=whole(6), out_specs=whole(13)
    )(*computed)
    return tuple(
        jnp.swapaxes(item, 0, 1) if i >= 3 and item.ndim == 3 else item for i, item in enumerate(final)
    )


def solution(mesh):
    latents = P(("dp", "fsdp"), None, None)
    rows = P(None, ("dp", "fsdp"), None)
    entries = P(None, ("dp", "fsdp"))
    weights = (rows, entries) * 5
    return jax.shard_map(
        local,
        mesh=mesh,
        in_specs=(latents, P(("dp", "fsdp"), None), *weights, latents),
        out_specs=(latents, latents, P(("dp", "fsdp"), None), *weights),
        check_vma=False,
    )
```
